512 devices in a mesh: ctx: 64 (over y_hi, x, z), chan: 8 (over y_lo, core).
Axes of the slice: x: 4, y: 8 (y_hi: 2, y_lo: 4; y = y_hi * 4 + y_lo), z: 8, core: 2. Of those that a mesh axis runs over, the one named last changes fastest.
Arguments:
- gate_q: bfloat16 [16, 262144], P('chan', 'ctx'), may hold values from -6 to 6
- gate_k: bfloat16 [16, 262144], P('chan', 'ctx'), may hold values from -6 to 6
- values: bfloat16 [16, 262144], P('chan', 'ctx'), may hold values from -6 to 6
- filter_taps: float32 [262144], P('ctx'), may hold values from -6 to 6
- skip_gain: float32 [16], P('chan'), may hold values from 0.5 to 1.5
- cotangent: bfloat16 [16, 262144], P('chan', 'ctx'), may hold values from -6 to 6
Outputs:
- gated_output: bfloat16 [16, 262144], P('chan', 'ctx')
- grad_query: bfloat16 [16, 262144], P('chan', 'ctx')
- grad_key: bfloat16 [16, 262144], P('chan', 'ctx')
- grad_values: bfloat16 [16, 262144], P('chan', 'ctx')
- grad_filter: float32 [262144], P('ctx')
The draws below stay inside these ranges and needn't reach their ends.
All inputs are finite; a program needn't handle non-finite values.
Results may differ from the reference program's by a relative error of at most 0.0024.
Values sent between devices are 32-bit elements; how exact they have to be, the bound alone decides.
No kernel may reach another device: no remote copies, remote signals or barrier semaphores. Data moves between devices by JAX's collectives and lax.ppermute only.
A program may use at most 64 MiB of HBM per device.

```python
import jax
import jax.numpy as jnp

TOKENS = 262144
CHANNELS = 16


def shard_levels(stream_key, extent, cuts, low, largest):
    level = 1.0
    for axis_at, blocks in cuts:
        steps = jax.random.uniform(jax.random.fold_in(jax.random.fold_in(stream_key, 6), axis_at), (blocks,), jnp.float32, low / len(cuts), largest / len(cuts))
        level = level * jnp.repeat(jnp.exp(steps), extent[axis_at] // blocks).reshape((-1,) + (1,) * (len(extent) - 1 - axis_at))
    return level


def noise(rng, dims, width, reach, split=(), held_as=jnp.bfloat16):
    entries = width * jax.random.normal(rng, dims, jnp.float32)
    if split:
        entries = entries * shard_levels(rng, dims, split, -0.22, 0.18)
    return jnp.clip(entries, -reach, reach).astype(held_as)


def setup_inputs(seed: int = 0) -> dict:
    splits = jax.random.split(jax.random.key(seed), 7)
    gate_q = noise(splits[0], (CHANNELS, TOKENS), 1.0, 6.0, ((0, 8), (1, 64)))
    gate_k = noise(splits[1], (CHANNELS, TOKENS), 1.0, 6.0, ((0, 8), (1, 64)))
    values = noise(splits[2], (CHANNELS, TOKENS), 1.0, 6.0, ((0, 8), (1, 64)))
    filter_taps = noise(splits[3], (TOKENS,), 1.0, 6.0, ((0, 64),), jnp.float32)
    skip_gain = jnp.clip(0.5 + 1.0 * jax.random.uniform(splits[4], (CHANNELS,), jnp.float32) ** shard_levels(splits[4], (CHANNELS,), ((0, 8),), -0.2, 0.2), 0.5, 1.5)
    cotangent = noise(splits[5], (CHANNELS, TOKENS), 1.0, 6.0, ((0, 8), (1, 64)))
    return dict(gate_q=gate_q, gate_k=gate_k, values=values, filter_taps=filter_taps, skip_gain=skip_gain, cotangent=cotangent)


def reference(gate_q, gate_k, values, filter_taps, skip_gain, cotangent):
    query = gate_q.astype(jnp.float32)
    key_gate = gate_k.astype(jnp.float32)
    value_in = values.astype(jnp.float32)
    cot = cotangent.astype(jnp.float32)
    fft_len = 2 * TOKENS
    filt_scale = TOKENS ** -0.5
    mixed = key_gate * value_in
    mixed_spec = jnp.fft.rfft(mixed, n=fft_len, axis=-1)
    filter_spec = jnp.fft.rfft(filter_taps, n=fft_len) * filt_scale
    conv = jnp.fft.irfft(mixed_spec * filter_spec[None, :], n=fft_len, axis=-1)[:, :TOKENS]
    summed = conv + skip_gain[:, None] * mixed
    gated_output = (query * summed).astype(jnp.bfloat16)
    grad_summed = cot * query
    grad_query = (cot * summed).astype(jnp.bfloat16)
    grad_spec = jnp.fft.rfft(grad_summed, n=fft_len, axis=-1)
    grad_mixed = jnp.fft.irfft(grad_spec * jnp.conj(filter_spec)[None, :], n=fft_len, axis=-1)[:, :TOKENS]
    grad_mixed = grad_mixed + skip_gain[:, None] * grad_summed
    grad_key = (grad_mixed * value_in).astype(jnp.bfloat16)
    grad_values = (grad_mixed * key_gate).astype(jnp.bfloat16)
    filter_total = jnp.sum(jnp.conj(mixed_spec) * grad_spec, axis=0)
    grad_filter = jnp.fft.irfft(filter_total, n=fft_len)[:TOKENS] * filt_scale
    return gated_output, grad_query, grad_key, grad_values, grad_filter
```

```python
import numpy as np

import jax
import jax.numpy as jnp
from jax import lax
from jax.experimental import pallas as pl
from jax.experimental.pallas import tpu as pltpu
from jax.sharding import PartitionSpec as P

BLOCK = 4096
BLOCKS = 64
ROWS = 32
LANES = 128
HALF = 64
SIGNALS = 5
WIDTH = SIGNALS * LANES


def split(value):
    high = value.astype(jnp.bfloat16)
    return high, (value - high.astype(jnp.float32)).astype(jnp.bfloat16)


def split_table(table):
    high = table.astype(np.float32).astype(jnp.bfloat16)
    low = (table - high.astype(np.float64)).astype(np.float32).astype(jnp.bfloat16)
    return high, low


def make_tables():
    a = np.arange(ROWS)
    b = np.arange(LANES)
    first = np.exp(-2j * np.pi * (a[:, None] * a[None, :] / ROWS + LANES * a[None, :] / (4 * BLOCK)))
    high, low = split_table(np.concatenate([first.real, first.imag], 0))
    first_table = np.concatenate([high, low, high], 1)
    last = np.conj(first.T) / BLOCK / (BLOCK * BLOCKS) ** 0.5
    high, low = split_table(np.concatenate([last.real, -last.imag], 1))
    last_table = np.concatenate([high, low, high], 1)
    twiddle = np.exp(-2j * np.pi * b[None, :] * (4 * a[:, None] + 1) / (4 * BLOCK))
    twiddle = np.stack([twiddle.real, twiddle.imag]).astype(np.float32)
    angle = 2 * np.pi * (b[:, None] * b[None, :] % LANES) / LANES
    cos, sin = np.cos(angle), np.sin(angle)
    real = np.concatenate([cos, sin], 0)
    imag = np.concatenate([-sin, cos], 0)
    order = [real[:, :HALF], imag[:, :HALF], real[:, HALF:], imag[:, HALF:]]
    second = np.concatenate(order, 1)
    return first_table, last_table, twiddle, split_table(second), split_table(second.T)


def dot(left, right):
    return jnp.dot(left, right, preferred_element_type=jnp.float32)


def dot3(value, high, low):
    value_high, value_low = split(value)
    return dot(value_high, high) + (dot(value_high, low) + dot(value_low, high))


def forward_kernel(
    key_ref, values_ref, cot_ref, query_ref, taps_ref, first_ref, twiddle_ref, high_ref, low_ref, out_ref, rows_ref
):
    f32 = jnp.float32
    mixed = key_ref[...].astype(f32) * values_ref[...].astype(f32)
    grad = cot_ref[...].astype(f32) * query_ref[...].astype(f32)
    for j in range(ROWS):
        cols = slice(LANES * j, LANES * (j + 1))
        rows_ref[0:2, j, :] = mixed[:, cols]
        rows_ref[2:4, j, :] = grad[:, cols]
    signals = [rows_ref[s] for s in range(4)] + [taps_ref[...]]
    high, low = split(jnp.concatenate(signals, 1))
    spread = dot(first_ref[...], jnp.concatenate([high, high, low], 0))
    tw_re, tw_im = twiddle_ref[0], twiddle_ref[1]
    turned = []
    for s in range(SIGNALS):
        cols = slice(LANES * s, LANES * (s + 1))
        re, im = spread[:ROWS, cols], spread[ROWS:, cols]
        turned.append(jnp.concatenate([re * tw_re - im * tw_im, re * tw_im + im * tw_re], 1))
    spectra = dot3(jnp.concatenate(turned, 0), high_ref[...], low_ref[...])
    for s in range(SIGNALS):
        for h in range(2):
            out_ref[ROWS * h : ROWS * (h + 1), 0, LANES * s : LANES * (s + 1)] = spectra[
                ROWS * s : ROWS * (s + 1), LANES * h : LANES * (h + 1)
            ]


def blocks_kernel(in_ref, out_ref, past_ref, next_ref, coef_ref, corr_ref):
    real_lane = lax.broadcasted_iota(jnp.int32, (BLOCKS, LANES), 1) < HALF
    zeros = jnp.zeros((BLOCKS, LANES), jnp.float32)

    def signal(s):
        return in_ref[:, 0, LANES * s : LANES * (s + 1)]

    def swap(value):
        return pltpu.roll(value, HALF, 1)

    taps = signal(4)
    corr_ref[0:8] = zeros[:8]
    corr_ref[8:72] = taps
    before = swap(corr_ref[7:71])
    taps = taps + jnp.where(real_lane, -before, before)
    swapped = swap(taps)
    coef_ref[0] = jnp.where(real_lane, taps, swapped)
    coef_ref[1] = jnp.where(real_lane, -swapped, taps)
    for c in range(2):
        mixed, grad = signal(c), signal(2 + c)
        mixed_swap = swap(mixed)
        past_ref[2 * c, 0:BLOCKS] = zeros
        past_ref[2 * c, BLOCKS:] = mixed
        past_ref[2 * c + 1, 0:BLOCKS] = zeros
        past_ref[2 * c + 1, BLOCKS:] = mixed_swap
        next_ref[2 * c, 0:BLOCKS] = grad
        next_ref[2 * c, BLOCKS:] = zeros
        next_ref[2 * c + 1, 0:BLOCKS] = swap(grad)
        next_ref[2 * c + 1, BLOCKS:] = zeros
        coef_ref[2 + 2 * c] = jnp.where(real_lane, mixed, mixed_swap)
        coef_ref[3 + 2 * c] = jnp.where(real_lane, mixed_swap, -mixed)

    for r in range(BLOCKS // 8):
        rows = slice(8 * r, 8 * r + 8)
        conv0 = conv1 = jnp.zeros((8, LANES), jnp.float32)
        for j in range(8 * r + 8):
            window = slice(BLOCKS + 8 * r - j, BLOCKS + 8 * r - j + 8)
            fa, fb = coef_ref[0, j : j + 1, :], coef_ref[1, j : j + 1, :]
            conv0 += fa * past_ref[0, window, :] + fb * past_ref[1, window, :]
            conv1 += fa * past_ref[2, window, :] + fb * past_ref[3, window, :]
        out_ref[rows, 0, 0:LANES] = conv0
        out_ref[rows, 0, LANES : 2 * LANES] = conv1
        grad0 = grad1 = corr = jnp.zeros((8, LANES), jnp.float32)
        for j in range(BLOCKS - 8 * r):
            window = slice(8 * r + j, 8 * r + j + 8)
            fa, fb = coef_ref[0, j : j + 1, :], coef_ref[1, j : j + 1, :]
            g0, g0s = next_ref[0, window, :], next_ref[1, window, :]
            g1, g1s = next_ref[2, window, :], next_ref[3, window, :]
            grad0 += fa * g0 - fb * g0s
            grad1 += fa * g1 - fb * g1s
            corr += coef_ref[2, j : j + 1, :] * g0 + coef_ref[3, j : j + 1, :] * g0s
            corr += coef_ref[4, j : j + 1, :] * g1 + coef_ref[5, j : j + 1, :] * g1s
        out_ref[rows, 0, 2 * LANES : 3 * LANES] = grad0
        out_ref[rows, 0, 3 * LANES : 4 * LANES] = grad1
        corr_ref[rows] = corr
    corr_ref[BLOCKS:] = zeros[:8]
    after = swap(corr_ref[1 : BLOCKS + 1])
    out_ref[:, 0, 4 * LANES :] = corr_ref[:BLOCKS] + jnp.where(real_lane, after, -after)


def inverse_kernel(
    in_ref, query_ref, key_ref, values_ref, cot_ref, gain_ref, last_ref, twiddle_ref, high_ref, low_ref,
    out_ref, grad_query_ref, grad_key_ref, grad_values_ref, grad_filter_ref, rows_ref,
):
    f32, bf16 = jnp.float32, jnp.bfloat16
    spectra = []
    for s in range(SIGNALS):
        cols = slice(LANES * s, LANES * (s + 1))
        spectra.append(jnp.concatenate([in_ref[:ROWS, 0, cols], in_ref[ROWS:, 0, cols]], 1))
    spread = dot3(jnp.concatenate(spectra, 0), high_ref[...], low_ref[...])
    tw_re, tw_im = twiddle_ref[0], twiddle_ref[1]
    real, imag = [], []
    for s in range(SIGNALS):
        re, im = spread[ROWS * s : ROWS * (s + 1), :LANES], spread[ROWS * s : ROWS * (s + 1), LANES:]
        real.append(re * tw_re + im * tw_im)
        imag.append(im * tw_re - re * tw_im)
    turned = jnp.concatenate([jnp.concatenate(real, 1), jnp.concatenate(imag, 1)], 0)
    high, low = split(turned)
    result = dot(last_ref[...], jnp.concatenate([high, high, low], 0))
    for s in range(4):
        rows_ref[s] = result[:, LANES * s : LANES * (s + 1)]
    grad_filter = result[:, 4 * LANES :]
    for copy in range(grad_filter_ref.shape[0]):
        grad_filter_ref[copy] = grad_filter
    gain = gain_ref[...]
    for j in range(ROWS):
        cols = slice(LANES * j, LANES * (j + 1))
        query, cot = query_ref[:, cols].astype(f32), cot_ref[:, cols].astype(f32)
        key, value = key_ref[:, cols].astype(f32), values_ref[:, cols].astype(f32)
        summed = rows_ref[0:2, j, :] + gain * (key * value)
        out_ref[:, cols] = (query * summed).astype(bf16)
        grad_query_ref[:, cols] = (cot * summed).astype(bf16)
        grad_mixed = rows_ref[2:4, j, :] + gain * (cot * query)
        grad_key_ref[:, cols] = (grad_mixed * value).astype(bf16)
        grad_values_ref[:, cols] = (grad_mixed * key).astype(bf16)


def per_device(gate_q, gate_k, values, filter_taps, skip_gain, cotangent):
    f32 = jnp.float32
    first, last, twiddle, second, second_back = jax.tree.map(jnp.asarray, make_tables())
    groups = lax.axis_size("chan")
    traffic = jax.ShapeDtypeStruct((BLOCKS, 1, WIDTH), f32)
    sent = pl.pallas_call(
        forward_kernel,
        out_shape=traffic,
        scratch_shapes=[pltpu.VMEM((4, ROWS, LANES), f32)],
        name="forward_transform",
    )(gate_k, values, cotangent, gate_q, filter_taps.reshape(ROWS, LANES), first, twiddle, *second)
    blocks = lax.all_to_all(sent, "ctx", 0, 0, tiled=True)
    sent = pl.pallas_call(
        blocks_kernel,
        out_shape=traffic,
        scratch_shapes=[
            pltpu.VMEM((4, 2 * BLOCKS, LANES), f32),
            pltpu.VMEM((4, 2 * BLOCKS, LANES), f32),
            pltpu.VMEM((6, BLOCKS, LANES), f32),
            pltpu.VMEM((BLOCKS + 8, LANES), f32),
        ],
        name="block_convolutions",
    )(blocks)
    spectra = lax.all_to_all(sent, "ctx", 0, 0, tiled=True)
    like = jax.ShapeDtypeStruct(gate_q.shape, jnp.bfloat16)
    *gated, partial_filter = pl.pallas_call(
        inverse_kernel,
        out_shape=(like, like, like, like, jax.ShapeDtypeStruct((groups, ROWS, LANES), f32)),
        scratch_shapes=[pltpu.VMEM((4, ROWS, LANES), f32)],
        name="inverse_transform",
    )(spectra, gate_q, gate_k, values, cotangent, skip_gain[:, None], last, twiddle, *second_back)
    grad_filter = jnp.sum(lax.all_to_all(partial_filter, "chan", 0, 0, tiled=True), axis=0)
    return (*gated, grad_filter.reshape(BLOCK))


def solution(mesh):
    return jax.shard_map(
        per_device,
        mesh=mesh,
        in_specs=(
            P("chan", "ctx"),
            P("chan", "ctx"),
            P("chan", "ctx"),
            P("ctx"),
            P("chan"),
            P("chan", "ctx"),
        ),
        out_specs=(
            P("chan", "ctx"),
            P("chan", "ctx"),
            P("chan", "ctx"),
            P("chan", "ctx"),
            P("ctx"),
        ),
        check_vma=False,
    )
```

```python
import numpy as np

import jax
import jax.numpy as jnp
from jax import lax
from jax.experimental import pallas as pl
from jax.experimental.pallas import tpu as pltpu
from jax.sharding import PartitionSpec as P

BLOCK = 4096
BLOCKS = 64
ROWS = 32
LANES = 128
HALF = 64
SIGNALS = 5
WIDTH = SIGNALS * LANES
FAR = 52
CTX_ORDER = [[FAR if p == 0 else 0 if p == FAR else p for p in range(BLOCKS)]]
CHAN_ORDER = [[4, 5, 2, 3, 6, 7, 0, 1]]


def split(value):
    high = value.astype(jnp.bfloat16)
    return high, (value - high.astype(jnp.float32)).astype(jnp.bfloat16)


def split_table(table):
    high = table.astype(np.float32).astype(jnp.bfloat16)
    low = (table - high.astype(np.float64)).astype(np.float32).astype(jnp.bfloat16)
    return high, low


def make_tables():
    a = np.arange(ROWS)
    b = np.arange(LANES)
    first = np.exp(-2j * np.pi * (a[:, None] * a[None, :] / ROWS + LANES * a[None, :] / (4 * BLOCK)))
    high, low = split_table(np.concatenate([first.real, first.imag], 0))
    first_table = np.concatenate([high, low, high], 1)
    last = np.conj(first.T) / BLOCK / (BLOCK * BLOCKS) ** 0.5
    high, low = split_table(np.concatenate([last.real, -last.imag], 1))
    last_table = np.concatenate([high, low, high], 1)
    twiddle = np.exp(-2j * np.pi * b[None, :] * (4 * a[:, None] + 1) / (4 * BLOCK))
    twiddle = np.stack([twiddle.real, twiddle.imag]).astype(np.float32)
    angle = 2 * np.pi * (b[:, None] * b[None, :] % LANES) / LANES
    cos, sin = np.cos(angle), np.sin(angle)
    real = np.concatenate([cos, sin], 0)
    imag = np.concatenate([-sin, cos], 0)
    order = [real[:, :HALF], imag[:, :HALF], real[:, HALF:], imag[:, HALF:]]
    second = np.concatenate(order, 1)
    return first_table, last_table, twiddle, split_table(second), split_table(second.T)


def dot(left, right):
    return jnp.dot(left, right, preferred_element_type=jnp.float32)


def dot3(value, high, low):
    value_high, value_low = split(value)
    return dot(value_high, high) + (dot(value_high, low) + dot(value_low, high))


def forward_kernel(
    key_ref, values_ref, cot_ref, query_ref, taps_ref, first_ref, twiddle_ref, high_ref, low_ref, out_ref, rows_ref
):
    f32 = jnp.float32
    mixed = key_ref[...].astype(f32) * values_ref[...].astype(f32)
    grad = cot_ref[...].astype(f32) * query_ref[...].astype(f32)
    for j in range(ROWS):
        cols = slice(LANES * j, LANES * (j + 1))
        rows_ref[0:2, j, :] = mixed[:, cols]
        rows_ref[2:4, j, :] = grad[:, cols]
    signals = [rows_ref[s] for s in range(4)] + [taps_ref[...]]
    high, low = split(jnp.concatenate(signals, 1))
    spread = dot(first_ref[...], jnp.concatenate([high, high, low], 0))
    tw_re, tw_im = twiddle_ref[0], twiddle_ref[1]
    turned = []
    for s in range(SIGNALS):
        cols = slice(LANES * s, LANES * (s + 1))
        re, im = spread[:ROWS, cols], spread[ROWS:, cols]
        turned.append(jnp.concatenate([re * tw_re - im * tw_im, re * tw_im + im * tw_re], 1))
    spectra = dot3(jnp.concatenate(turned, 0), high_ref[...], low_ref[...])
    for s in range(SIGNALS):
        for h in range(2):
            out_ref[ROWS * h : ROWS * (h + 1), 0, LANES * s : LANES * (s + 1)] = spectra[
                ROWS * s : ROWS * (s + 1), LANES * h : LANES * (h + 1)
            ]


def blocks_kernel(in_ref, out_ref, past_ref, next_ref, coef_ref, corr_ref):
    real_lane = lax.broadcasted_iota(jnp.int32, (BLOCKS, LANES), 1) < HALF
    zeros = jnp.zeros((BLOCKS, LANES), jnp.float32)

    def signal(s):
        cols = slice(LANES * s, LANES * (s + 1))
        return jnp.concatenate([in_ref[FAR : FAR + 1, 0, cols], in_ref[1:FAR, 0, cols], in_ref[0:1, 0, cols], in_ref[FAR + 1 :, 0, cols]], 0)

    def put(first, value, s):
        cols = slice(LANES * s, LANES * (s + 1))
        if first == 0:
            out_ref[FAR : FAR + 1, 0, cols] = value[0:1]
            out_ref[1:8, 0, cols] = value[1:8]
        elif first <= FAR < first + 8:
            at = FAR - first
            out_ref[first:FAR, 0, cols] = value[:at]
            out_ref[0:1, 0, cols] = value[at : at + 1]
            out_ref[FAR + 1 : first + 8, 0, cols] = value[at + 1 :]
        else:
            out_ref[first : first + 8, 0, cols] = value

    def swap(value):
        return pltpu.roll(value, HALF, 1)

    taps = signal(4)
    corr_ref[0:8] = zeros[:8]
    corr_ref[8:72] = taps
    before = swap(corr_ref[7:71])
    taps = taps + jnp.where(real_lane, -before, before)
    swapped = swap(taps)
    coef_ref[0] = jnp.where(real_lane, taps, swapped)
    coef_ref[1] = jnp.where(real_lane, -swapped, taps)
    for c in range(2):
        mixed, grad = signal(c), signal(2 + c)
        mixed_swap = swap(mixed)
        past_ref[2 * c, 0:BLOCKS] = zeros
        past_ref[2 * c, BLOCKS:] = mixed
        past_ref[2 * c + 1, 0:BLOCKS] = zeros
        past_ref[2 * c + 1, BLOCKS:] = mixed_swap
        next_ref[2 * c, 0:BLOCKS] = grad
        next_ref[2 * c, BLOCKS:] = zeros
        next_ref[2 * c + 1, 0:BLOCKS] = swap(grad)
        next_ref[2 * c + 1, BLOCKS:] = zeros
        coef_ref[2 + 2 * c] = jnp.where(real_lane, mixed, mixed_swap)
        coef_ref[3 + 2 * c] = jnp.where(real_lane, mixed_swap, -mixed)

    for r in range(BLOCKS // 8):
        rows = slice(8 * r, 8 * r + 8)
        conv0 = conv1 = jnp.zeros((8, LANES), jnp.float32)
        for j in range(8 * r + 8):
            window = slice(BLOCKS + 8 * r - j, BLOCKS + 8 * r - j + 8)
            fa, fb = coef_ref[0, j : j + 1, :], coef_ref[1, j : j + 1, :]
            conv0 += fa * past_ref[0, window, :] + fb * past_ref[1, window, :]
            conv1 += fa * past_ref[2, window, :] + fb * past_ref[3, window, :]
        put(8 * r, conv0, 0)
        put(8 * r, conv1, 1)
        grad0 = grad1 = corr = jnp.zeros((8, LANES), jnp.float32)
        for j in range(BLOCKS - 8 * r):
            window = slice(8 * r + j, 8 * r + j + 8)
            fa, fb = coef_ref[0, j : j + 1, :], coef_ref[1, j : j + 1, :]
            g0, g0s = next_ref[0, window, :], next_ref[1, window, :]
            g1, g1s = next_ref[2, window, :], next_ref[3, window, :]
            grad0 += fa * g0 - fb * g0s
            grad1 += fa * g1 - fb * g1s
            corr += coef_ref[2, j : j + 1, :] * g0 + coef_ref[3, j : j + 1, :] * g0s
            corr += coef_ref[4, j : j + 1, :] * g1 + coef_ref[5, j : j + 1, :] * g1s
        put(8 * r, grad0, 2)
        put(8 * r, grad1, 3)
        corr_ref[rows] = corr
    corr_ref[BLOCKS:] = zeros[:8]
    after = swap(corr_ref[1 : BLOCKS + 1])
    taps_grad = corr_ref[:BLOCKS] + jnp.where(real_lane, after, -after)
    for r in range(BLOCKS // 8):
        put(8 * r, taps_grad[8 * r : 8 * r + 8], 4)


def inverse_kernel(
    in_ref, query_ref, key_ref, values_ref, cot_ref, gain_ref, last_ref, twiddle_ref, high_ref, low_ref,
    out_ref, grad_query_ref, grad_key_ref, grad_values_ref, grad_filter_ref, rows_ref,
):
    f32, bf16 = jnp.float32, jnp.bfloat16
    spectra = []
    for s in range(SIGNALS):
        cols = slice(LANES * s, LANES * (s + 1))
        spectra.append(jnp.concatenate([in_ref[:ROWS, 0, cols], in_ref[ROWS:, 0, cols]], 1))
    spread = dot3(jnp.concatenate(spectra, 0), high_ref[...], low_ref[...])
    tw_re, tw_im = twiddle_ref[0], twiddle_ref[1]
    real, imag = [], []
    for s in range(SIGNALS):
        re, im = spread[ROWS * s : ROWS * (s + 1), :LANES], spread[ROWS * s : ROWS * (s + 1), LANES:]
        real.append(re * tw_re + im * tw_im)
        imag.append(im * tw_re - re * tw_im)
    turned = jnp.concatenate([jnp.concatenate(real, 1), jnp.concatenate(imag, 1)], 0)
    high, low = split(turned)
    result = dot(last_ref[...], jnp.concatenate([high, high, low], 0))
    for s in range(4):
        rows_ref[s] = result[:, LANES * s : LANES * (s + 1)]
    grad_filter = result[:, 4 * LANES :]
    for copy in range(grad_filter_ref.shape[0]):
        grad_filter_ref[copy] = grad_filter
    first_channel = lax.broadcasted_iota(jnp.int32, (2, LANES), 0) == 0
    gain = jnp.where(first_channel, gain_ref[0], gain_ref[1])
    for j in range(ROWS):
        cols = slice(LANES * j, LANES * (j + 1))
        query, cot = query_ref[:, cols].astype(f32), cot_ref[:, cols].astype(f32)
        key, value = key_ref[:, cols].astype(f32), values_ref[:, cols].astype(f32)
        summed = rows_ref[0:2, j, :] + gain * (key * value)
        out_ref[:, cols] = (query * summed).astype(bf16)
        grad_query_ref[:, cols] = (cot * summed).astype(bf16)
        grad_mixed = rows_ref[2:4, j, :] + gain * (cot * query)
        grad_key_ref[:, cols] = (grad_mixed * value).astype(bf16)
        grad_values_ref[:, cols] = (grad_mixed * key).astype(bf16)


def per_device(gate_q, gate_k, values, filter_taps, skip_gain, cotangent):
    f32 = jnp.float32
    first, last, twiddle, second, second_back = jax.tree.map(jnp.asarray, make_tables())
    groups = lax.axis_size("chan")
    traffic = jax.ShapeDtypeStruct((BLOCKS, 1, WIDTH), f32)
    sent = pl.pallas_call(
        forward_kernel,
        out_shape=traffic,
        scratch_shapes=[pltpu.VMEM((4, ROWS, LANES), f32)],
        name="forward_transform",
    )(gate_k, values, cotangent, gate_q, filter_taps.reshape(ROWS, LANES), first, twiddle, *second)
    blocks = lax.all_to_all(sent, "ctx", 0, 0, tiled=True, axis_index_groups=CTX_ORDER)
    sent = pl.pallas_call(
        blocks_kernel,
        out_shape=traffic,
        scratch_shapes=[
            pltpu.VMEM((4, 2 * BLOCKS, LANES), f32),
            pltpu.VMEM((4, 2 * BLOCKS, LANES), f32),
            pltpu.VMEM((6, BLOCKS, LANES), f32),
            pltpu.VMEM((BLOCKS + 8, LANES), f32),
        ],
        name="block_convolutions",
    )(blocks)
    spectra = lax.all_to_all(sent, "ctx", 0, 0, tiled=True, axis_index_groups=CTX_ORDER)
    vmem = pl.BlockSpec(memory_space=pltpu.VMEM)
    like = jax.ShapeDtypeStruct(gate_q.shape, jnp.bfloat16)
    *gated, partial_filter = pl.pallas_call(
        inverse_kernel,
        out_shape=(like, like, like, like, jax.ShapeDtypeStruct((groups, ROWS, LANES), f32)),
        in_specs=[vmem] * 5 + [pl.BlockSpec(memory_space=pltpu.SMEM)] + [vmem] * 4,
        scratch_shapes=[pltpu.VMEM((4, ROWS, LANES), f32)],
        name="inverse_transform",
    )(spectra, gate_q, gate_k, values, cotangent, skip_gain, last, twiddle, *second_back)
    grad_filter = jnp.sum(lax.all_to_all(partial_filter, "chan", 0, 0, tiled=True, axis_index_groups=CHAN_ORDER), axis=0)
    return (*gated, grad_filter.reshape(BLOCK))


def solution(mesh):
    return jax.shard_map(
        per_device,
        mesh=mesh,
        in_specs=(
            P("chan", "ctx"),
            P("chan", "ctx"),
            P("chan", "ctx"),
            P("ctx"),
            P("chan"),
            P("chan", "ctx"),
        ),
        out_specs=(
            P("chan", "ctx"),
            P("chan", "ctx"),
            P("chan", "ctx"),
            P("chan", "ctx"),
            P("ctx"),
        ),
        check_vma=False,
    )
```

```python
import numpy as np

import jax
import jax.numpy as jnp
from jax import lax
from jax.experimental import pallas as pl
from jax.experimental.pallas import tpu as pltpu
from jax.sharding import PartitionSpec as P

BLOCK = 4096
BLOCKS = 64
ROWS = 32
LANES = 128
HALF = 64
SIGNALS = 5
WIDTH = SIGNALS * LANES
SMALL = pltpu.CompilerParams(vmem_limit_bytes=8 << 20)
FAR = 52
CTX_ORDER = [[FAR if p == 0 else 0 if p == FAR else p for p in range(BLOCKS)]]
CHAN_ORDER = [[4, 5, 2, 3, 6, 7, 0, 1]]


def split(value):
    high = value.astype(jnp.bfloat16)
    return high, (value - high.astype(jnp.float32)).astype(jnp.bfloat16)


def split_table(table):
    high = table.astype(np.float32).astype(jnp.bfloat16)
    low = (table - high.astype(np.float64)).astype(np.float32).astype(jnp.bfloat16)
    return high, low


def make_tables():
    a = np.arange(ROWS)
    b = np.arange(LANES)
    first = np.exp(-2j * np.pi * (a[:, None] * a[None, :] / ROWS + LANES * a[None, :] / (4 * BLOCK)))
    high, low = split_table(np.concatenate([first.real, first.imag], 0))
    first_table = np.concatenate([high, low, high], 1)
    last = np.conj(first.T) / BLOCK / (BLOCK * BLOCKS) ** 0.5
    high, low = split_table(np.concatenate([last.real, -last.imag], 1))
    last_table = np.concatenate([high, low, high], 1)
    twiddle = np.exp(-2j * np.pi * b[None, :] * (4 * a[:, None] + 1) / (4 * BLOCK))
    twiddle = np.stack([twiddle.real, twiddle.imag]).astype(np.float32)
    angle = 2 * np.pi * (b[:, None] * b[None, :] % LANES) / LANES
    cos, sin = np.cos(angle), np.sin(angle)
    real = np.concatenate([cos, sin], 0)
    imag = np.concatenate([-sin, cos], 0)
    order = [real[:, :HALF], imag[:, :HALF], real[:, HALF:], imag[:, HALF:]]
    second = np.concatenate(order, 1)
    return first_table, last_table, twiddle, split_table(second), split_table(second.T)


def dot(left, right):
    return jnp.dot(left, right, preferred_element_type=jnp.float32)


def dot3(value, high, low):
    value_high, value_low = split(value)
    return dot(value_high, high) + (dot(value_high, low) + dot(value_low, high))


def forward_kernel(
    key_ref, values_ref, cot_ref, query_ref, taps_ref, first_ref, twiddle_ref, high_ref, low_ref, out_ref, rows_ref
):
    f32 = jnp.float32
    mixed = key_ref[...].astype(f32) * values_ref[...].astype(f32)
    grad = cot_ref[...].astype(f32) * query_ref[...].astype(f32)
    for j in range(ROWS):
        cols = slice(LANES * j, LANES * (j + 1))
        rows_ref[0:2, j, :] = mixed[:, cols]
        rows_ref[2:4, j, :] = grad[:, cols]
    signals = [rows_ref[s] for s in range(4)] + [taps_ref[...]]
    high, low = split(jnp.concatenate(signals, 1))
    spread = dot(first_ref[...], jnp.concatenate([high, high, low], 0))
    tw_re, tw_im = twiddle_ref[0], twiddle_ref[1]
    turned = []
    for s in range(SIGNALS):
        cols = slice(LANES * s, LANES * (s + 1))
        re, im = spread[:ROWS, cols], spread[ROWS:, cols]
        turned.append(jnp.concatenate([re * tw_re - im * tw_im, re * tw_im + im * tw_re], 1))
    spectra = dot3(jnp.concatenate(turned, 0), high_ref[...], low_ref[...])
    for s in range(SIGNALS):
        for h in range(2):
            out_ref[ROWS * h : ROWS * (h + 1), 0, LANES * s : LANES * (s + 1)] = spectra[
                ROWS * s : ROWS * (s + 1), LANES * h : LANES * (h + 1)
            ]


def blocks_kernel(in_ref, out_ref, past_ref, next_ref, coef_ref, corr_ref):
    real_lane = lax.broadcasted_iota(jnp.int32, (BLOCKS, LANES), 1) < HALF
    zeros = jnp.zeros((BLOCKS, LANES), jnp.float32)

    def signal(s):
        cols = slice(LANES * s, LANES * (s + 1))
        return jnp.concatenate([in_ref[FAR : FAR + 1, 0, cols], in_ref[1:FAR, 0, cols], in_ref[0:1, 0, cols], in_ref[FAR + 1 :, 0, cols]], 0)

    def put(first, value, s):
        cols = slice(LANES * s, LANES * (s + 1))
        if first == 0:
            out_ref[FAR : FAR + 1, 0, cols] = value[0:1]
            out_ref[1:8, 0, cols] = value[1:8]
        elif first <= FAR < first + 8:
            at = FAR - first
            out_ref[first:FAR, 0, cols] = value[:at]
            out_ref[0:1, 0, cols] = value[at : at + 1]
            out_ref[FAR + 1 : first + 8, 0, cols] = value[at + 1 :]
        else:
            out_ref[first : first + 8, 0, cols] = value

    def swap(value):
        return pltpu.roll(value, HALF, 1)

    taps = signal(4)
    corr_ref[0:8] = zeros[:8]
    corr_ref[8:72] = taps
    before = swap(corr_ref[7:71])
    taps = taps + jnp.where(real_lane, -before, before)
    swapped = swap(taps)
    coef_ref[0] = jnp.where(real_lane, taps, swapped)
    coef_ref[1] = jnp.where(real_lane, -swapped, taps)
    for c in range(2):
        mixed, grad = signal(c), signal(2 + c)
        mixed_swap = swap(mixed)
        past_ref[2 * c, 0:BLOCKS] = zeros
        past_ref[2 * c, BLOCKS:] = mixed
        past_ref[2 * c + 1, 0:BLOCKS] = zeros
        past_ref[2 * c + 1, BLOCKS:] = mixed_swap
        next_ref[2 * c, 0:BLOCKS] = grad
        next_ref[2 * c, BLOCKS:] = zeros
        next_ref[2 * c + 1, 0:BLOCKS] = swap(grad)
        next_ref[2 * c + 1, BLOCKS:] = zeros
        coef_ref[2 + 2 * c] = jnp.where(real_lane, mixed, mixed_swap)
        coef_ref[3 + 2 * c] = jnp.where(real_lane, mixed_swap, -mixed)

    for r in range(BLOCKS // 8):
        rows = slice(8 * r, 8 * r + 8)
        conv0 = conv1 = jnp.zeros((8, LANES), jnp.float32)
        for j in range(8 * r + 8):
            window = slice(BLOCKS + 8 * r - j, BLOCKS + 8 * r - j + 8)
            fa, fb = coef_ref[0, j : j + 1, :], coef_ref[1, j : j + 1, :]
            conv0 += fa * past_ref[0, window, :] + fb * past_ref[1, window, :]
            conv1 += fa * past_ref[2, window, :] + fb * past_ref[3, window, :]
        put(8 * r, conv0, 0)
        put(8 * r, conv1, 1)
        grad0 = grad1 = corr = jnp.zeros((8, LANES), jnp.float32)
        for j in range(BLOCKS - 8 * r):
            window = slice(8 * r + j, 8 * r + j + 8)
            fa, fb = coef_ref[0, j : j + 1, :], coef_ref[1, j : j + 1, :]
            g0, g0s = next_ref[0, window, :], next_ref[1, window, :]
            g1, g1s = next_ref[2, window, :], next_ref[3, window, :]
            grad0 += fa * g0 - fb * g0s
            grad1 += fa * g1 - fb * g1s
            corr += coef_ref[2, j : j + 1, :] * g0 + coef_ref[3, j : j + 1, :] * g0s
            corr += coef_ref[4, j : j + 1, :] * g1 + coef_ref[5, j : j + 1, :] * g1s
        put(8 * r, grad0, 2)
        put(8 * r, grad1, 3)
        corr_ref[rows] = corr
    corr_ref[BLOCKS:] = zeros[:8]
    after = swap(corr_ref[1 : BLOCKS + 1])
    taps_grad = corr_ref[:BLOCKS] + jnp.where(real_lane, after, -after)
    for r in range(BLOCKS // 8):
        put(8 * r, taps_grad[8 * r : 8 * r + 8], 4)


def inverse_kernel(
    in_ref, query_ref, key_ref, values_ref, cot_ref, gain_ref, last_ref, twiddle_ref, high_ref, low_ref,
    out_ref, grad_query_ref, grad_key_ref, grad_values_ref, grad_filter_ref, rows_ref,
):
    f32, bf16 = jnp.float32, jnp.bfloat16
    spectra = []
    for s in range(SIGNALS):
        cols = slice(LANES * s, LANES * (s + 1))
        spectra.append(jnp.concatenate([in_ref[:ROWS, 0, cols], in_ref[ROWS:, 0, cols]], 1))
    spread = dot3(jnp.concatenate(spectra, 0), high_ref[...], low_ref[...])
    tw_re, tw_im = twiddle_ref[0], twiddle_ref[1]
    real, imag = [], []
    for s in range(SIGNALS):
        re, im = spread[ROWS * s : ROWS * (s + 1), :LANES], spread[ROWS * s : ROWS * (s + 1), LANES:]
        real.append(re * tw_re + im * tw_im)
        imag.append(im * tw_re - re * tw_im)
    turned = jnp.concatenate([jnp.concatenate(real, 1), jnp.concatenate(imag, 1)], 0)
    high, low = split(turned)
    result = dot(last_ref[...], jnp.concatenate([high, high, low], 0))
    for s in range(4):
        rows_ref[s] = result[:, LANES * s : LANES * (s + 1)]
    grad_filter = result[:, 4 * LANES :]
    for copy in range(grad_filter_ref.shape[0]):
        grad_filter_ref[copy] = grad_filter
    first_channel = lax.broadcasted_iota(jnp.int32, (2, LANES), 0) == 0
    gain = jnp.where(first_channel, gain_ref[0], gain_ref[1])
    for j in range(ROWS):
        cols = slice(LANES * j, LANES * (j + 1))
        query, cot = query_ref[:, cols].astype(f32), cot_ref[:, cols].astype(f32)
        key, value = key_ref[:, cols].astype(f32), values_ref[:, cols].astype(f32)
        summed = rows_ref[0:2, j, :] + gain * (key * value)
        out_ref[:, cols] = (query * summed).astype(bf16)
        grad_query_ref[:, cols] = (cot * summed).astype(bf16)
        grad_mixed = rows_ref[2:4, j, :] + gain * (cot * query)
        grad_key_ref[:, cols] = (grad_mixed * value).astype(bf16)
        grad_values_ref[:, cols] = (grad_mixed * key).astype(bf16)


def per_device(gate_q, gate_k, values, filter_taps, skip_gain, cotangent):
    f32 = jnp.float32
    first, last, twiddle, second, second_back = jax.tree.map(jnp.asarray, make_tables())
    groups = lax.axis_size("chan")
    traffic = jax.ShapeDtypeStruct((BLOCKS, 1, WIDTH), f32)
    sent = pl.pallas_call(
        forward_kernel,
        out_shape=traffic,
        scratch_shapes=[pltpu.VMEM((4, ROWS, LANES), f32)],
        compiler_params=SMALL,
        name="forward_transform",
    )(gate_k, values, cotangent, gate_q, filter_taps.reshape(ROWS, LANES), first, twiddle, *second)
    blocks = lax.all_to_all(sent, "ctx", 0, 0, tiled=True, axis_index_groups=CTX_ORDER)
    sent = pl.pallas_call(
        blocks_kernel,
        out_shape=traffic,
        scratch_shapes=[
            pltpu.VMEM((4, 2 * BLOCKS, LANES), f32),
            pltpu.VMEM((4, 2 * BLOCKS, LANES), f32),
            pltpu.VMEM((6, BLOCKS, LANES), f32),
            pltpu.VMEM((BLOCKS + 8, LANES), f32),
        ],
        compiler_params=SMALL,
        name="block_convolutions",
    )(blocks)
    spectra = lax.all_to_all(sent, "ctx", 0, 0, tiled=True, axis_index_groups=CTX_ORDER)
    vmem = pl.BlockSpec(memory_space=pltpu.VMEM)
    like = jax.ShapeDtypeStruct(gate_q.shape, jnp.bfloat16)
    *gated, partial_filter = pl.pallas_call(
        inverse_kernel,
        out_shape=(like, like, like, like, jax.ShapeDtypeStruct((groups, ROWS, LANES), f32)),
        in_specs=[vmem] * 5 + [pl.BlockSpec(memory_space=pltpu.SMEM)] + [vmem] * 4,
        scratch_shapes=[pltpu.VMEM((4, ROWS, LANES), f32)],
        compiler_params=SMALL,
        name="inverse_transform",
    )(spectra, gate_q, gate_k, values, cotangent, skip_gain, last, twiddle, *second_back)
    grad_filter = jnp.sum(lax.all_to_all(partial_filter, "chan", 0, 0, tiled=True, axis_index_groups=CHAN_ORDER), axis=0)
    return (*gated, grad_filter.reshape(BLOCK))


def solution(mesh):
    return jax.shard_map(
        per_device,
        mesh=mesh,
        in_specs=(
            P("chan", "ctx"),
            P("chan", "ctx"),
            P("chan", "ctx"),
            P("ctx"),
            P("chan"),
            P("chan", "ctx"),
        ),
        out_specs=(
            P("chan", "ctx"),
            P("chan", "ctx"),
            P("chan", "ctx"),
            P("chan", "ctx"),
            P("ctx"),
        ),
        check_vma=False,
    )
```

```python
import numpy as np

import jax
import jax.numpy as jnp
from jax import lax
from jax.experimental import pallas as pl
from jax.experimental.pallas import tpu as pltpu
from jax.sharding import PartitionSpec as P

BLOCK = 4096
BLOCKS = 64
ROWS = 32
LANES = 128
HALF = 64
SIGNALS = 5
WIDTH = SIGNALS * LANES
SMALL = pltpu.CompilerParams(vmem_limit_bytes=8 << 20)
FAR = 52
CTX_ORDER = [[FAR if p == 0 else 0 if p == FAR else p for p in range(BLOCKS)]]
CHAN_ORDER = [[4, 5, 2, 3, 6, 7, 0, 1]]


def split(value):
    high = value.astype(jnp.bfloat16)
    return high, (value - high.astype(jnp.float32)).astype(jnp.bfloat16)


def split_table(table):
    high = table.astype(np.float32).astype(jnp.bfloat16)
    low = (table - high.astype(np.float64)).astype(np.float32).astype(jnp.bfloat16)
    return high, low


def make_tables():
    a = np.arange(ROWS)
    b = np.arange(LANES)
    first = np.exp(-2j * np.pi * (a[:, None] * a[None, :] / ROWS + LANES * a[None, :] / (4 * BLOCK)))
    high, low = split_table(np.concatenate([first.real, first.imag], 0))
    first_table = np.concatenate([high, low, high], 1)
    last = np.conj(first.T) / BLOCK / (BLOCK * BLOCKS) ** 0.5
    high, low = split_table(np.concatenate([last.real, -last.imag], 1))
    last_table = np.concatenate([high, low, high], 1)
    twiddle = np.exp(-2j * np.pi * b[None, :] * (4 * a[:, None] + 1) / (4 * BLOCK))
    twiddle = np.stack([twiddle.real, twiddle.imag]).astype(np.float32)
    angle = 2 * np.pi * (b[:, None] * b[None, :] % LANES) / LANES
    cos, sin = np.cos(angle), np.sin(angle)
    real = np.concatenate([cos, sin], 0)
    imag = np.concatenate([-sin, cos], 0)
    order = [real[:, :HALF], imag[:, :HALF], real[:, HALF:], imag[:, HALF:]]
    second = np.concatenate(order, 1)
    return first_table, last_table, twiddle, split_table(second), split_table(second.T)


def make_block_tables():
    blocks = np.array(CTX_ORDER[0])
    phases = np.arange(2 * BLOCKS)
    wave = np.exp(-2j * np.pi * phases[:, None] * blocks[None, :] / (2 * BLOCKS))
    step = np.exp(-2j * np.pi * phases / (2 * BLOCKS))
    back = np.conj(wave.T) / (2 * BLOCKS)

    def there(table):
        high, low = split_table(np.concatenate([table.real, -table.imag], 0))
        return np.concatenate([high, low, high], 1)

    def here(table):
        return split_table(np.concatenate([table.real, table.imag], 1))

    filter_wave = wave * (1 + 1j * step)[:, None]
    filter_back = back * (1 - 1j * np.conj(step))[None, :]
    return there(wave), there(filter_wave), *here(back), *here(filter_back)


def dot(left, right):
    return jnp.dot(left, right, preferred_element_type=jnp.float32)


def dot3(value, high, low):
    value_high, value_low = split(value)
    return dot(value_high, high) + (dot(value_high, low) + dot(value_low, high))


def forward_kernel(*refs):
    operands, (out_ref, *held, rows_ref, sems) = refs[:9], refs[9:]
    copies = [pltpu.make_async_copy(src, dst, sems.at[n]) for n, (src, dst) in enumerate(zip(operands, held))]
    for copy in copies:
        copy.start()
    for copy in copies:
        copy.wait()
    key_ref, values_ref, cot_ref, query_ref, taps_ref, first_ref, twiddle_ref, high_ref, low_ref = held
    f32 = jnp.float32
    mixed = key_ref[...].astype(f32) * values_ref[...].astype(f32)
    grad = cot_ref[...].astype(f32) * query_ref[...].astype(f32)
    for j in range(ROWS):
        cols = slice(LANES * j, LANES * (j + 1))
        rows_ref[0:2, j, :] = mixed[:, cols]
        rows_ref[2:4, j, :] = grad[:, cols]
    signals = [rows_ref[s] for s in range(4)] + [taps_ref[...]]
    high, low = split(jnp.concatenate(signals, 1))
    spread = dot(first_ref[...], jnp.concatenate([high, high, low], 0))
    tw_re, tw_im = twiddle_ref[0], twiddle_ref[1]
    turned = []
    for s in range(SIGNALS):
        cols = slice(LANES * s, LANES * (s + 1))
        re, im = spread[:ROWS, cols], spread[ROWS:, cols]
        turned.append(jnp.concatenate([re * tw_re - im * tw_im, re * tw_im + im * tw_re], 1))
    spectra = dot3(jnp.concatenate(turned, 0), high_ref[...], low_ref[...])
    for s in range(SIGNALS):
        for h in range(2):
            out_ref[ROWS * h : ROWS * (h + 1), 0, LANES * s : LANES * (s + 1)] = spectra[
                ROWS * s : ROWS * (s + 1), LANES * h : LANES * (h + 1)
            ]


def swap(value):
    return pltpu.roll(value, HALF, 1)


def blocks_kernel(in_ref, there_ref, filter_there_ref, high_ref, low_ref, filter_high_ref, filter_low_ref, out_ref):
    real = lax.broadcasted_iota(jnp.int32, (2 * BLOCKS, LANES), 1) < HALF

    def spectra(table_ref, signals):
        high, low = split(jnp.concatenate([in_ref[:, 0, LANES * s : LANES * (s + 1)] for s in signals], 1))
        terms = dot(table_ref[...], jnp.concatenate([high, high, low], 0))
        result = []
        for n in range(len(signals)):
            cols = slice(LANES * n, LANES * (n + 1))
            sine = swap(terms[2 * BLOCKS :, cols])
            result.append(terms[: 2 * BLOCKS, cols] + jnp.where(real, sine, -sine))
        return result

    def turn(value):
        swapped = swap(value)
        return jnp.where(real, -swapped, swapped)

    def blocks(table_high_ref, table_low_ref, values):
        cosine, sine = jnp.concatenate(values, 1), jnp.concatenate([turn(v) for v in values], 1)
        high, low = split(jnp.concatenate([cosine, sine], 0))
        table_high = table_high_ref[...]
        return dot(table_high, high) + (dot(table_high, low) + dot(table_low_ref[...], high))

    (taps,) = spectra(filter_there_ref, [4])
    mixed0, mixed1, grad0, grad1 = spectra(there_ref, range(4))
    taps_swap = swap(taps)
    both_real, both_imag = jnp.where(real, taps, taps_swap), jnp.where(real, -taps_swap, taps)
    results, corr = [], None
    for mixed in (mixed0, mixed1):
        results.append(both_real * mixed + both_imag * swap(mixed))
    for mixed, grad in ((mixed0, grad0), (mixed1, grad1)):
        grad_swap, mixed_swap = swap(grad), swap(mixed)
        results.append(both_real * grad - both_imag * grad_swap)
        product = jnp.where(real, mixed, mixed_swap) * grad + jnp.where(real, mixed_swap, -mixed) * grad_swap
        corr = product if corr is None else corr + product
    out_ref[:, 0, : 4 * LANES] = blocks(high_ref, low_ref, results)
    out_ref[:, 0, 4 * LANES :] = blocks(filter_high_ref, filter_low_ref, [corr])


def inverse_kernel(
    in_ref, query_ref, key_ref, values_ref, cot_ref, gain_ref, last_ref, twiddle_ref, high_ref, low_ref,
    out_ref, grad_query_ref, grad_key_ref, grad_values_ref, grad_filter_ref, rows_ref,
):
    f32, bf16 = jnp.float32, jnp.bfloat16
    spectra = []
    for s in range(SIGNALS):
        cols = slice(LANES * s, LANES * (s + 1))
        spectra.append(jnp.concatenate([in_ref[:ROWS, 0, cols], in_ref[ROWS:, 0, cols]], 1))
    spread = dot3(jnp.concatenate(spectra, 0), high_ref[...], low_ref[...])
    tw_re, tw_im = twiddle_ref[0], twiddle_ref[1]
    real, imag = [], []
    for s in range(SIGNALS):
        re, im = spread[ROWS * s : ROWS * (s + 1), :LANES], spread[ROWS * s : ROWS * (s + 1), LANES:]
        real.append(re * tw_re + im * tw_im)
        imag.append(im * tw_re - re * tw_im)
    turned = jnp.concatenate([jnp.concatenate(real, 1), jnp.concatenate(imag, 1)], 0)
    high, low = split(turned)
    result = dot(last_ref[...], jnp.concatenate([high, high, low], 0))
    for s in range(4):
        rows_ref[s] = result[:, LANES * s : LANES * (s + 1)]
    grad_filter = result[:, 4 * LANES :]
    for copy in range(grad_filter_ref.shape[0]):
        grad_filter_ref[copy] = grad_filter
    first_channel = lax.broadcasted_iota(jnp.int32, (2, LANES), 0) == 0
    gain = jnp.where(first_channel, gain_ref[0], gain_ref[1])
    for j in range(ROWS):
        cols = slice(LANES * j, LANES * (j + 1))
        query, cot = query_ref[:, cols].astype(f32), cot_ref[:, cols].astype(f32)
        key, value = key_ref[:, cols].astype(f32), values_ref[:, cols].astype(f32)
        summed = rows_ref[0:2, j, :] + gain * (key * value)
        out_ref[:, cols] = (query * summed).astype(bf16)
        grad_query_ref[:, cols] = (cot * summed).astype(bf16)
        grad_mixed = rows_ref[2:4, j, :] + gain * (cot * query)
        grad_key_ref[:, cols] = (grad_mixed * value).astype(bf16)
        grad_values_ref[:, cols] = (grad_mixed * key).astype(bf16)


def per_device(gate_q, gate_k, values, filter_taps, skip_gain, cotangent):
    f32 = jnp.float32
    first, last, twiddle, second, second_back = jax.tree.map(jnp.asarray, make_tables())
    groups = lax.axis_size("chan")
    traffic = jax.ShapeDtypeStruct((BLOCKS, 1, WIDTH), f32)
    vmem = pl.BlockSpec(memory_space=pltpu.VMEM)
    operands = (gate_k, values, cotangent, gate_q, filter_taps.reshape(ROWS, LANES), first, twiddle, *second)
    sent = pl.pallas_call(
        forward_kernel,
        out_shape=traffic,
        in_specs=[pl.BlockSpec(memory_space=pltpu.HBM)] * len(operands),
        scratch_shapes=[
            *(pltpu.VMEM(v.shape, v.dtype) for v in operands),
            pltpu.VMEM((4, ROWS, LANES), f32),
            pltpu.SemaphoreType.DMA((len(operands),)),
        ],
        compiler_params=SMALL,
        name="forward_transform",
    )(*operands)
    blocks = lax.all_to_all(sent, "ctx", 0, 0, tiled=True, axis_index_groups=CTX_ORDER)
    sent = pl.pallas_call(
        blocks_kernel,
        out_shape=traffic,
        compiler_params=SMALL,
        name="block_convolutions",
    )(blocks, *jax.tree.map(jnp.asarray, make_block_tables()))
    spectra = lax.all_to_all(sent, "ctx", 0, 0, tiled=True, axis_index_groups=CTX_ORDER)
    like = jax.ShapeDtypeStruct(gate_q.shape, jnp.bfloat16)
    *gated, partial_filter = pl.pallas_call(
        inverse_kernel,
        out_shape=(like, like, like, like, jax.ShapeDtypeStruct((groups, ROWS, LANES), f32)),
        in_specs=[vmem] * 5 + [pl.BlockSpec(memory_space=pltpu.SMEM)] + [vmem] * 4,
        scratch_shapes=[pltpu.VMEM((4, ROWS, LANES), f32)],
        compiler_params=SMALL,
        name="inverse_transform",
    )(spectra, gate_q, gate_k, values, cotangent, skip_gain, last, twiddle, *second_back)
    grad_filter = jnp.sum(lax.all_to_all(partial_filter, "chan", 0, 0, tiled=True, axis_index_groups=CHAN_ORDER), axis=0)
    return (*gated, grad_filter.reshape(BLOCK))


def solution(mesh):
    return jax.shard_map(
        per_device,
        mesh=mesh,
        in_specs=(
            P("chan", "ctx"),
            P("chan", "ctx"),
            P("chan", "ctx"),
            P("ctx"),
            P("chan"),
            P("chan", "ctx"),
        ),
        out_specs=(
            P("chan", "ctx"),
            P("chan", "ctx"),
            P("chan", "ctx"),
            P("chan", "ctx"),
            P("ctx"),
        ),
        check_vma=False,
    )
```

```python
import numpy as np

import jax
import jax.numpy as jnp
from jax import lax
from jax.experimental import pallas as pl
from jax.experimental.pallas import tpu as pltpu
from jax.sharding import PartitionSpec as P

BLOCK = 4096
BLOCKS = 64
ROWS = 32
LANES = 128
HALF = 64
SIGNALS = 5
WIDTH = SIGNALS * LANES
SMALL = pltpu.CompilerParams(vmem_limit_bytes=8 << 20)
FAR = 52
CTX_ORDER = [[FAR if p == 0 else 0 if p == FAR else p for p in range(BLOCKS)]]
CHAN_ORDER = [[4, 5, 2, 3, 6, 7, 0, 1]]


def split(value):
    high = value.astype(jnp.bfloat16)
    return high, (value - high.astype(jnp.float32)).astype(jnp.bfloat16)


def split_table(table):
    high = table.astype(np.float32).astype(jnp.bfloat16)
    low = (table - high.astype(np.float64)).astype(np.float32).astype(jnp.bfloat16)
    return high, low


def make_tables():
    a = np.arange(ROWS)
    b = np.arange(LANES)
    first = np.exp(-2j * np.pi * (a[:, None] * a[None, :] / ROWS + LANES * a[None, :] / (4 * BLOCK)))
    high, low = split_table(np.concatenate([first.real, first.imag], 0))
    first_table = np.concatenate([high, low, high], 1)
    last = np.conj(first.T) / BLOCK / (BLOCK * BLOCKS) ** 0.5
    high, low = split_table(np.concatenate([last.real, -last.imag], 1))
    last_table = np.concatenate([high, low, high], 1)
    twiddle = np.exp(-2j * np.pi * b[None, :] * (4 * a[:, None] + 1) / (4 * BLOCK))
    twiddle = np.stack([twiddle.real, twiddle.imag]).astype(np.float32)
    angle = 2 * np.pi * (b[:, None] * b[None, :] % LANES) / LANES
    cos, sin = np.cos(angle), np.sin(angle)
    real = np.concatenate([cos, sin], 0)
    imag = np.concatenate([-sin, cos], 0)
    order = [real[:, :HALF], imag[:, :HALF], real[:, HALF:], imag[:, HALF:]]
    second = np.concatenate(order, 1)
    return first_table, last_table, twiddle, split_table(second), split_table(second.T)


def make_block_tables():
    blocks = np.array(CTX_ORDER[0])
    phases = np.arange(2 * BLOCKS)
    wave = np.exp(-2j * np.pi * phases[:, None] * blocks[None, :] / (2 * BLOCKS))
    step = np.exp(-2j * np.pi * phases / (2 * BLOCKS))
    back = np.conj(wave.T) / (2 * BLOCKS)

    def there(table):
        high, low = split_table(np.concatenate([table.real, -table.imag], 0))
        return np.concatenate([high, low, high], 1)

    def here(table):
        return split_table(np.concatenate([table.real, table.imag], 1))

    filter_wave = wave * (1 + 1j * step)[:, None]
    filter_back = back * (1 - 1j * np.conj(step))[None, :]
    return there(wave), there(filter_wave), *here(back), *here(filter_back)


def dot(left, right):
    return jnp.dot(left, right, preferred_element_type=jnp.float32)


def dot3(value, high, low):
    value_high, value_low = split(value)
    return dot(value_high, high) + (dot(value_high, low) + dot(value_low, high))


def forward_kernel(*refs):
    operands, (out_ref, *held, rows_ref, sems) = refs[:9], refs[9:]
    copies = [pltpu.make_async_copy(src, dst, sems.at[n]) for n, (src, dst) in enumerate(zip(operands, held))]
    for copy in copies:
        copy.start()
    for copy in copies:
        copy.wait()
    key_ref, values_ref, cot_ref, query_ref, taps_ref, first_ref, twiddle_ref, high_ref, low_ref = held
    f32 = jnp.float32
    mixed = key_ref[...].astype(f32) * values_ref[...].astype(f32)
    grad = cot_ref[...].astype(f32) * query_ref[...].astype(f32)
    for j in range(ROWS):
        cols = slice(LANES * j, LANES * (j + 1))
        rows_ref[0:2, j, :] = mixed[:, cols]
        rows_ref[2:4, j, :] = grad[:, cols]
    signals = [rows_ref[s] for s in range(4)] + [taps_ref[...]]
    high, low = split(jnp.concatenate(signals, 1))
    spread = dot(first_ref[...], jnp.concatenate([high, high, low], 0))
    tw_re, tw_im = twiddle_ref[0], twiddle_ref[1]
    turned = []
    for s in range(SIGNALS):
        cols = slice(LANES * s, LANES * (s + 1))
        re, im = spread[:ROWS, cols], spread[ROWS:, cols]
        turned.append(jnp.concatenate([re * tw_re - im * tw_im, re * tw_im + im * tw_re], 1))
    spectra = dot3(jnp.concatenate(turned, 0), high_ref[...], low_ref[...])
    for s in range(SIGNALS):
        for h in range(2):
            out_ref[ROWS * h : ROWS * (h + 1), 0, LANES * s : LANES * (s + 1)] = spectra[
                ROWS * s : ROWS * (s + 1), LANES * h : LANES * (h + 1)
            ]


def swap(value):
    return pltpu.roll(value, HALF, 1)


def blocks_kernel(in_ref, there_ref, filter_there_ref, high_ref, low_ref, filter_high_ref, filter_low_ref, out_ref):
    real = lax.broadcasted_iota(jnp.int32, (2 * BLOCKS, LANES), 1) < HALF

    def spectra(table_ref, signals):
        high, low = split(jnp.concatenate([in_ref[:, 0, LANES * s : LANES * (s + 1)] for s in signals], 1))
        terms = dot(table_ref[...], jnp.concatenate([high, high, low], 0))
        result = []
        for n in range(len(signals)):
            cols = slice(LANES * n, LANES * (n + 1))
            sine = swap(terms[2 * BLOCKS :, cols])
            result.append(terms[: 2 * BLOCKS, cols] + jnp.where(real, sine, -sine))
        return result

    def turn(value):
        swapped = swap(value)
        return jnp.where(real, -swapped, swapped)

    def blocks(table_high_ref, table_low_ref, values):
        cosine, sine = jnp.concatenate(values, 1), jnp.concatenate([turn(v) for v in values], 1)
        high, low = split(jnp.concatenate([cosine, sine], 0))
        table_high = table_high_ref[...]
        return dot(table_high, high) + (dot(table_high, low) + dot(table_low_ref[...], high))

    (taps,) = spectra(filter_there_ref, [4])
    mixed0, mixed1, grad0, grad1 = spectra(there_ref, range(4))
    taps_swap = swap(taps)
    both_real, both_imag = jnp.where(real, taps, taps_swap), jnp.where(real, -taps_swap, taps)
    results, corr = [], None
    for mixed in (mixed0, mixed1):
        results.append(both_real * mixed + both_imag * swap(mixed))
    for mixed, grad in ((mixed0, grad0), (mixed1, grad1)):
        grad_swap, mixed_swap = swap(grad), swap(mixed)
        results.append(both_real * grad - both_imag * grad_swap)
        product = jnp.where(real, mixed, mixed_swap) * grad + jnp.where(real, mixed_swap, -mixed) * grad_swap
        corr = product if corr is None else corr + product
    out_ref[:, 0, : 4 * LANES] = blocks(high_ref, low_ref, results)
    out_ref[:, 0, 4 * LANES :] = blocks(filter_high_ref, filter_low_ref, [corr])


def inverse_kernel(
    in_ref, query_ref, key_ref, values_ref, cot_ref, gain_ref, last_ref, twiddle_ref, high_ref, low_ref,
    out_ref, grad_query_ref, grad_key_ref, grad_values_ref, grad_filter_ref, rows_ref,
):
    f32, bf16 = jnp.float32, jnp.bfloat16
    spectra = []
    for s in range(SIGNALS):
        cols = slice(LANES * s, LANES * (s + 1))
        spectra.append(jnp.concatenate([in_ref[:ROWS, 0, cols], in_ref[ROWS:, 0, cols]], 1))
    spread = dot3(jnp.concatenate(spectra, 0), high_ref[...], low_ref[...])
    tw_re, tw_im = twiddle_ref[0], twiddle_ref[1]
    real, imag = [], []
    for s in range(SIGNALS):
        re, im = spread[ROWS * s : ROWS * (s + 1), :LANES], spread[ROWS * s : ROWS * (s + 1), LANES:]
        real.append(re * tw_re + im * tw_im)
        imag.append(im * tw_re - re * tw_im)
    turned = jnp.concatenate([jnp.concatenate(real, 1), jnp.concatenate(imag, 1)], 0)
    high, low = split(turned)
    result = dot(last_ref[...], jnp.concatenate([high, high, low], 0))
    for s in range(4):
        rows_ref[s] = result[:, LANES * s : LANES * (s + 1)]
    grad_filter = result[:, 4 * LANES :]
    for copy in range(grad_filter_ref.shape[0]):
        grad_filter_ref[copy] = grad_filter
    first_channel = lax.broadcasted_iota(jnp.int32, (2, LANES), 0) == 0
    gain = jnp.where(first_channel, gain_ref[0], gain_ref[1])
    for j in range(ROWS):
        cols = slice(LANES * j, LANES * (j + 1))
        query, cot = query_ref[:, cols].astype(f32), cot_ref[:, cols].astype(f32)
        key, value = key_ref[:, cols].astype(f32), values_ref[:, cols].astype(f32)
        summed = rows_ref[0:2, j, :] + gain * (key * value)
        out_ref[:, cols] = (query * summed).astype(bf16)
        grad_query_ref[:, cols] = (cot * summed).astype(bf16)
        grad_mixed = rows_ref[2:4, j, :] + gain * (cot * query)
        grad_key_ref[:, cols] = (grad_mixed * value).astype(bf16)
        grad_values_ref[:, cols] = (grad_mixed * key).astype(bf16)


def per_device(gate_q, gate_k, values, filter_taps, skip_gain, cotangent):
    f32 = jnp.float32
    first, last, twiddle, second, second_back = jax.tree.map(jnp.asarray, make_tables())
    groups = lax.axis_size("chan")
    traffic = jax.ShapeDtypeStruct((BLOCKS, 1, WIDTH), f32)
    vmem = pl.BlockSpec(memory_space=pltpu.VMEM)
    operands = (gate_k, values, cotangent, gate_q, filter_taps.reshape(ROWS, LANES), first, twiddle, *second)
    sent = pl.pallas_call(
        forward_kernel,
        out_shape=traffic,
        in_specs=[pl.BlockSpec(memory_space=pltpu.HBM)] * len(operands),
        scratch_shapes=[
            *(pltpu.VMEM(v.shape, v.dtype) for v in operands),
            pltpu.VMEM((4, ROWS, LANES), f32),
            pltpu.SemaphoreType.DMA((len(operands),)),
        ],
        compiler_params=SMALL,
        name="forward_transform",
    )(*(pltpu.with_memory_space_constraint(v, pltpu.HBM) for v in operands))
    blocks = lax.all_to_all(sent, "ctx", 0, 0, tiled=True, axis_index_groups=CTX_ORDER)
    sent = pl.pallas_call(
        blocks_kernel,
        out_shape=traffic,
        compiler_params=SMALL,
        name="block_convolutions",
    )(blocks, *jax.tree.map(jnp.asarray, make_block_tables()))
    spectra = lax.all_to_all(sent, "ctx", 0, 0, tiled=True, axis_index_groups=CTX_ORDER)
    like = jax.ShapeDtypeStruct(gate_q.shape, jnp.bfloat16)
    *gated, partial_filter = pl.pallas_call(
        inverse_kernel,
        out_shape=(like, like, like, like, jax.ShapeDtypeStruct((groups, ROWS, LANES), f32)),
        in_specs=[vmem] * 5 + [pl.BlockSpec(memory_space=pltpu.SMEM)] + [vmem] * 4,
        scratch_shapes=[pltpu.VMEM((4, ROWS, LANES), f32)],
        compiler_params=SMALL,
        name="inverse_transform",
    )(spectra, gate_q, gate_k, values, cotangent, skip_gain, last, twiddle, *second_back)
    grad_filter = jnp.sum(lax.all_to_all(partial_filter, "chan", 0, 0, tiled=True, axis_index_groups=CHAN_ORDER), axis=0)
    return (*gated, grad_filter.reshape(BLOCK))


def solution(mesh):
    return jax.shard_map(
        per_device,
        mesh=mesh,
        in_specs=(
            P("chan", "ctx"),
            P("chan", "ctx"),
            P("chan", "ctx"),
            P("ctx"),
            P("chan"),
            P("chan", "ctx"),
        ),
        out_specs=(
            P("chan", "ctx"),
            P("chan", "ctx"),
            P("chan", "ctx"),
            P("chan", "ctx"),
            P("ctx"),
        ),
        check_vma=False,
    )
```

```python
import numpy as np

import jax
import jax.numpy as jnp
from jax import lax
from jax.experimental import pallas as pl
from jax.experimental.pallas import tpu as pltpu
from jax.sharding import PartitionSpec as P

BLOCK = 4096
BLOCKS = 64
ROWS = 32
LANES = 128
HALVES = 32
SIGNALS = 5
PAIR = 2 * LANES
WIDTH = SIGNALS * PAIR
SMALL = pltpu.CompilerParams(vmem_limit_bytes=8 << 20)
CORNER = 20
PLANE_ORDER = [CORNER if p == 0 else 0 if p == CORNER else p for p in range(HALVES)]
CTX_ORDER = [[HALVES + p for p in PLANE_ORDER] + PLANE_ORDER]
HALF_ORDER = [PLANE_ORDER, [HALVES + p for p in PLANE_ORDER]]
CHAN_ORDER = [[5, 4, 2, 3, 6, 7, 0, 1]]


def split(value):
    high = value.astype(jnp.bfloat16)
    return high, (value - high.astype(jnp.float32)).astype(jnp.bfloat16)


def split_table(table):
    high = table.astype(np.float32).astype(jnp.bfloat16)
    low = (table - high.astype(np.float64)).astype(np.float32).astype(jnp.bfloat16)
    return high, low


def make_tables():
    a = np.arange(ROWS)
    b = np.arange(LANES)
    first = np.exp(-2j * np.pi * (a[:, None] * a[None, :] / ROWS + LANES * a[None, :] / (4 * BLOCK)))
    first = np.concatenate([first.real, first.imag], 0)
    first_pair = np.zeros((2, 2 * ROWS, ROWS, 2))
    first_pair[0, :, :, 0] = first_pair[1, :, :, 1] = first
    last = np.exp(2j * np.pi * (a[:, None] * a[None, :] / ROWS + LANES * a[:, None] / (4 * BLOCK)))
    last = np.concatenate([last.real, -last.imag], 1) / BLOCK / (BLOCK * BLOCKS) ** 0.5
    last_pair = np.zeros((ROWS, 2, 2, 2 * ROWS))
    last_pair[:, 0, 0] = last_pair[:, 1, 1] = last

    def thrice(table):
        high, low = split_table(table)
        return np.concatenate([high, low, high], 1)

    first_table = thrice(first_pair.reshape(4 * ROWS, 2 * ROWS)), thrice(first)
    last_table = thrice(last_pair.reshape(2 * ROWS, 4 * ROWS)), thrice(last)
    twiddle = np.exp(-2j * np.pi * b[None, :] * (4 * a[:, None] + 1) / (4 * BLOCK))
    twiddle = np.stack([twiddle.real, twiddle.imag]).astype(np.float32)
    angle = 2 * np.pi * (b[:, None] * b[None, :] % LANES) / LANES
    cos, sin = np.cos(angle), np.sin(angle)
    second = np.block([[cos, -sin], [sin, cos]])
    return first_table, last_table, twiddle, split_table(second), split_table(second.T)


def make_block_tables():
    blocks = np.array(CTX_ORDER[0])
    phases = np.arange(2 * BLOCKS)
    wave = np.exp(-2j * np.pi * phases[:, None] * blocks[None, :] / (2 * BLOCKS))
    step = np.exp(-2j * np.pi * phases / (2 * BLOCKS))
    back = np.conj(wave.T) / (2 * BLOCKS)

    def there(table):
        high, low = split_table(np.concatenate([table.real, -table.imag], 0))
        return np.concatenate([high, low, high], 1)

    def here(table):
        rows = [table[HALVES:], table[:HALVES]]
        return split_table(np.stack([np.concatenate([t.real, t.imag], 1) for t in rows]))

    filter_wave = wave * (1 + 1j * step)[:, None]
    filter_back = back * (1 - 1j * np.conj(step))[None, :]
    return there(wave), there(filter_wave), *here(back), *here(filter_back)


def dot(left, right):
    return jnp.dot(left, right, preferred_element_type=jnp.float32)


def dot3(value, high, low):
    value_high, value_low = split(value)
    rows = value.shape[0]
    both = dot(jnp.concatenate([value_high, value_low], 0), high)
    return both[:rows] + (dot(value_high, low) + both[rows:])


def stack3(value):
    high, low = split(value)
    return jnp.concatenate([high, high, low], 0)


def forward_kernel(*refs):
    operands, (out_ref, *held, sems) = refs[:10], refs[10:]
    copies = [pltpu.make_async_copy(src, dst, sems.at[n]) for n, (src, dst) in enumerate(zip(operands, held))]
    for copy in copies:
        copy.start()
    key_ref, values_ref, cot_ref, query_ref, taps_ref, pair_ref, first_ref, twiddle_ref, high_ref, low_ref = held
    f32 = jnp.float32
    for copy in copies[:5]:
        copy.wait()
    mixed = key_ref[...].astype(f32) * values_ref[...].astype(f32)
    grad = cot_ref[...].astype(f32) * query_ref[...].astype(f32)
    pairs, taps = stack3(jnp.concatenate([mixed, grad], 1)), stack3(taps_ref[...])
    for copy in copies[5:7]:
        copy.wait()
    pairs, taps = dot(pair_ref[...], pairs), dot(first_ref[...], taps)
    copies[7].wait()
    tw_re, tw_im = twiddle_ref[0], twiddle_ref[1]
    places = [(pairs, 0, 0), (pairs, 1, 0), (pairs, 0, 1), (pairs, 1, 1), (taps, 0, 0)]
    turned = []
    for spread, row, col in places:
        cols = slice(LANES * col, LANES * (col + 1))
        re = spread[2 * ROWS * row : 2 * ROWS * row + ROWS, cols]
        im = spread[2 * ROWS * row + ROWS : 2 * ROWS * (row + 1), cols]
        turned.append(jnp.concatenate([re * tw_re - im * tw_im, re * tw_im + im * tw_re], 1))
    for copy in copies[8:]:
        copy.wait()
    spectra = dot3(jnp.concatenate(turned, 0), high_ref[...], low_ref[...])
    for s in range(SIGNALS):
        for h in range(2):
            out_ref[HALVES * h : HALVES * (h + 1), 0, PAIR * s : PAIR * (s + 1)] = spectra[ROWS * s : ROWS * (s + 1)]


def blocks_kernel(in_ref, there_ref, filter_there_ref, high_ref, low_ref, filter_high_ref, filter_low_ref, out_ref):
    half = lax.axis_index("ctx") // HALVES

    def spectra(table_ref, signals):
        high, low = split(jnp.concatenate([in_ref[:, 0, PAIR * s : PAIR * (s + 1)] for s in signals], 1))
        terms = dot(table_ref[...], jnp.concatenate([high, high, low], 0))
        cosine, sine = terms[: 2 * BLOCKS], terms[2 * BLOCKS :]
        result = []
        for n in range(len(signals)):
            real, imag = slice(PAIR * n, PAIR * n + LANES), slice(PAIR * n + LANES, PAIR * (n + 1))
            result.append((cosine[:, real] + sine[:, imag], cosine[:, imag] - sine[:, real]))
        return result

    def blocks(table_high_ref, table_low_ref, values):
        cosine = jnp.concatenate([part for real, imag in values for part in (real, imag)], 1)
        sine = jnp.concatenate([part for real, imag in values for part in (-imag, real)], 1)
        high, low = split(jnp.concatenate([cosine, sine], 0))
        table_high = table_high_ref[half]
        both = dot(jnp.concatenate([table_high, table_low_ref[half]], 0), high)
        return both[:HALVES] + (dot(table_high, low) + both[HALVES:])

    ((taps_re, taps_im),) = spectra(filter_there_ref, [4])
    signals = spectra(there_ref, range(4))
    results, corr_re, corr_im = [], 0.0, 0.0
    for re, im in signals[:2]:
        results.append((taps_re * re - taps_im * im, taps_re * im + taps_im * re))
    for (mixed_re, mixed_im), (re, im) in zip(signals[:2], signals[2:]):
        results.append((taps_re * re + taps_im * im, taps_re * im - taps_im * re))
        corr_re += mixed_re * re + mixed_im * im
        corr_im += mixed_re * im - mixed_im * re
    out_ref[:, 0, : 4 * PAIR] = blocks(high_ref, low_ref, results)
    out_ref[:, 0, 4 * PAIR :] = blocks(filter_high_ref, filter_low_ref, [(corr_re, corr_im)])


def inverse_kernel(
    in_ref, query_ref, key_ref, values_ref, cot_ref, gain_ref, pair_ref, last_ref, twiddle_ref, high_ref, low_ref,
    out_ref, grad_query_ref, grad_key_ref, grad_values_ref, grad_filter_ref,
):
    f32, bf16 = jnp.float32, jnp.bfloat16
    spectra = jnp.concatenate([in_ref[:, 0, PAIR * s : PAIR * (s + 1)] for s in range(SIGNALS)], 0)
    spread = dot3(spectra, high_ref[...], low_ref[...])
    tw_re, tw_im = twiddle_ref[0], twiddle_ref[1]
    turned = []
    for s in range(SIGNALS):
        rows = slice(ROWS * s, ROWS * (s + 1))
        re, im = spread[rows, :LANES], spread[rows, LANES:]
        turned += [re * tw_re + im * tw_im, im * tw_re - re * tw_im]
    pairs = jnp.concatenate([jnp.concatenate(turned[:4], 0), jnp.concatenate(turned[4:8], 0)], 1)
    grad_filter = dot(last_ref[...], stack3(jnp.concatenate(turned[8:], 0)))
    for copy in range(grad_filter_ref.shape[0]):
        grad_filter_ref[copy] = grad_filter
    pairs = dot(pair_ref[...], stack3(pairs))
    query, cot = query_ref[...].astype(f32), cot_ref[...].astype(f32)
    key, value = key_ref[...].astype(f32), values_ref[...].astype(f32)
    first_channel = lax.broadcasted_iota(jnp.int32, query.shape, 0) % 2 == 0
    gain = jnp.where(first_channel, gain_ref[0], gain_ref[1])
    summed = pairs[:, :LANES] + gain * (key * value)
    out_ref[...] = (query * summed).astype(bf16)
    grad_query_ref[...] = (cot * summed).astype(bf16)
    grad_mixed = pairs[:, LANES:] + gain * (cot * query)
    grad_key_ref[...] = (grad_mixed * value).astype(bf16)
    grad_values_ref[...] = (grad_mixed * key).astype(bf16)


def by_rows(pair):
    return pair.reshape(2, ROWS, LANES).transpose(1, 0, 2).reshape(2 * ROWS, LANES)


def by_channel(rows):
    return rows.reshape(ROWS, 2, LANES).transpose(1, 0, 2).reshape(2, BLOCK)


def per_device(gate_q, gate_k, values, filter_taps, skip_gain, cotangent):
    f32 = jnp.float32
    first, last, twiddle, second, second_back = jax.tree.map(jnp.asarray, make_tables())
    groups = lax.axis_size("chan")
    gate_q, gate_k, values, cotangent = map(by_rows, (gate_q, gate_k, values, cotangent))
    vmem = pl.BlockSpec(memory_space=pltpu.VMEM)
    operands = (gate_k, values, cotangent, gate_q, filter_taps.reshape(ROWS, LANES), *first, twiddle, *second)
    sent = pl.pallas_call(
        forward_kernel,
        out_shape=jax.ShapeDtypeStruct((BLOCKS, 1, WIDTH), f32),
        in_specs=[pl.BlockSpec(memory_space=pltpu.HBM)] * len(operands),
        scratch_shapes=[
            *(pltpu.VMEM(v.shape, v.dtype) for v in operands),
            pltpu.SemaphoreType.DMA((len(operands),)),
        ],
        compiler_params=SMALL,
        name="forward_transform",
    )(*(pltpu.with_memory_space_constraint(v, pltpu.HBM) for v in operands))
    blocks = lax.all_to_all(sent, "ctx", 0, 0, tiled=True, axis_index_groups=CTX_ORDER)
    sent = pl.pallas_call(
        blocks_kernel,
        out_shape=jax.ShapeDtypeStruct((HALVES, 1, WIDTH), f32),
        compiler_params=SMALL,
        name="block_convolutions",
    )(blocks, *jax.tree.map(jnp.asarray, make_block_tables()))
    spectra = lax.all_to_all(sent, "ctx", 0, 0, tiled=True, axis_index_groups=HALF_ORDER)
    like = jax.ShapeDtypeStruct(gate_q.shape, jnp.bfloat16)
    *gated, partial_filter = pl.pallas_call(
        inverse_kernel,
        out_shape=(like, like, like, like, jax.ShapeDtypeStruct((groups, ROWS, LANES), f32)),
        in_specs=[vmem] * 5 + [pl.BlockSpec(memory_space=pltpu.SMEM)] + [vmem] * 5,
        compiler_params=SMALL,
        name="inverse_transform",
    )(spectra, gate_q, gate_k, values, cotangent, skip_gain, *last, twiddle, *second_back)
    partials = lax.all_to_all(partial_filter, "chan", 0, 0, tiled=True, axis_index_groups=CHAN_ORDER)
    grad_filter = jnp.sum(partials, axis=0)
    return (*map(by_channel, gated), grad_filter.reshape(BLOCK))


def solution(mesh):
    return jax.shard_map(
        per_device,
        mesh=mesh,
        in_specs=(
            P("chan", "ctx"),
            P("chan", "ctx"),
            P("chan", "ctx"),
            P("ctx"),
            P("chan"),
            P("chan", "ctx"),
        ),
        out_specs=(
            P("chan", "ctx"),
            P("chan", "ctx"),
            P("chan", "ctx"),
            P("chan", "ctx"),
            P("ctx"),
        ),
        check_vma=False,
    )
```

```python
import numpy as np

import jax
import jax.numpy as jnp
from jax import lax
from jax.experimental import pallas as pl
from jax.experimental.pallas import tpu as pltpu
from jax.sharding import PartitionSpec as P

BLOCK = 4096
BLOCKS = 64
ROWS = 32
LANES = 128
HALVES = 32
SIGNALS = 5
PAIR = 2 * LANES
WIDTH = SIGNALS * PAIR
SMALL = pltpu.CompilerParams(vmem_limit_bytes=8 << 20)
CORNER = 20
PLANE_ORDER = [CORNER if p == 0 else 0 if p == CORNER else p for p in range(HALVES)]
CTX_ORDER = [[HALVES + p for p in PLANE_ORDER] + PLANE_ORDER]
HALF_ORDER = [PLANE_ORDER, [HALVES + p for p in PLANE_ORDER]]
CHAN_ORDER = [[5, 4, 2, 3, 6, 7, 0, 1]]


def split(value):
    high = value.astype(jnp.bfloat16)
    return high, (value - high.astype(jnp.float32)).astype(jnp.bfloat16)


def split_table(table):
    high = table.astype(np.float32).astype(jnp.bfloat16)
    low = (table - high.astype(np.float64)).astype(np.float32).astype(jnp.bfloat16)
    return high, low


def make_tables():
    a = np.arange(ROWS)
    b = np.arange(LANES)
    first = np.exp(-2j * np.pi * (a[:, None] * a[None, :] / ROWS + LANES * a[None, :] / (4 * BLOCK)))
    first = np.concatenate([first.real, first.imag], 0)
    first_pair = np.zeros((2, 2 * ROWS, ROWS, 2))
    first_pair[0, :, :, 0] = first_pair[1, :, :, 1] = first
    last = np.exp(2j * np.pi * (a[:, None] * a[None, :] / ROWS + LANES * a[:, None] / (4 * BLOCK)))
    last = np.concatenate([last.real, -last.imag], 1) / BLOCK / (BLOCK * BLOCKS) ** 0.5
    last_pair = np.zeros((ROWS, 2, 2, 2 * ROWS))
    last_pair[:, 0, 0] = last_pair[:, 1, 1] = last

    def thrice(table):
        high, low = split_table(table)
        return np.concatenate([high, low, high], 1)

    first_table = thrice(first_pair.reshape(4 * ROWS, 2 * ROWS)), thrice(first)
    last_table = thrice(last_pair.reshape(2 * ROWS, 4 * ROWS)), thrice(last)
    twiddle = np.exp(-2j * np.pi * b[None, :] * (4 * a[:, None] + 1) / (4 * BLOCK))
    twiddle = np.stack([twiddle.real, twiddle.imag]).astype(np.float32)
    angle = 2 * np.pi * (b[:, None] * b[None, :] % LANES) / LANES
    cos, sin = np.cos(angle), np.sin(angle)
    second = np.block([[cos, -sin], [sin, cos]])
    return first_table, last_table, twiddle, split_table(second), split_table(second.T)


def make_block_tables():
    blocks = np.array(CTX_ORDER[0])
    phases = np.arange(2 * BLOCKS)
    wave = np.exp(-2j * np.pi * phases[:, None] * blocks[None, :] / (2 * BLOCKS))
    step = np.exp(-2j * np.pi * phases / (2 * BLOCKS))
    back = np.conj(wave.T) / (2 * BLOCKS)

    def there(table):
        high, low = split_table(np.concatenate([table.real, -table.imag], 0))
        return np.concatenate([high, low, high], 1)

    def here(table):
        rows = [table[HALVES:], table[:HALVES]]
        return split_table(np.stack([np.concatenate([t.real, t.imag], 1) for t in rows]))

    filter_wave = wave * (1 + 1j * step)[:, None]
    filter_back = back * (1 - 1j * np.conj(step))[None, :]
    return there(wave), there(filter_wave), *here(back), *here(filter_back)


def dot(left, right):
    return jnp.dot(left, right, preferred_element_type=jnp.float32)


def dot3(value, high, low):
    value_high, value_low = split(value)
    rows = value.shape[0]
    both = dot(jnp.concatenate([value_high, value_low], 0), high)
    return both[:rows] + (dot(value_high, low) + both[rows:])


def stack3(value):
    high, low = split(value)
    return jnp.concatenate([high, high, low], 0)


def forward_kernel(*refs):
    operands, (out_ref, *held, sems) = refs[:10], refs[10:]
    copies = [pltpu.make_async_copy(src, dst, sems.at[n]) for n, (src, dst) in enumerate(zip(operands, held))]
    for copy in copies:
        copy.start()
    key_ref, values_ref, cot_ref, query_ref, taps_ref, pair_ref, first_ref, twiddle_ref, high_ref, low_ref = held
    f32 = jnp.float32
    for copy in copies[:5]:
        copy.wait()
    mixed = key_ref[...].astype(f32) * values_ref[...].astype(f32)
    grad = cot_ref[...].astype(f32) * query_ref[...].astype(f32)
    pairs, taps = stack3(jnp.concatenate([mixed, grad], 1)), stack3(taps_ref[...])
    for copy in copies[5:7]:
        copy.wait()
    pairs, taps = dot(pair_ref[...], pairs), dot(first_ref[...], taps)
    copies[7].wait()
    tw_re, tw_im = twiddle_ref[0], twiddle_ref[1]
    places = [(pairs, 0, 0), (pairs, 1, 0), (pairs, 0, 1), (pairs, 1, 1), (taps, 0, 0)]
    turned = []
    for spread, row, col in places:
        cols = slice(LANES * col, LANES * (col + 1))
        re = spread[2 * ROWS * row : 2 * ROWS * row + ROWS, cols]
        im = spread[2 * ROWS * row + ROWS : 2 * ROWS * (row + 1), cols]
        turned.append(jnp.concatenate([re * tw_re - im * tw_im, re * tw_im + im * tw_re], 1))
    for copy in copies[8:]:
        copy.wait()
    spectra = dot3(jnp.concatenate(turned, 0), high_ref[...], low_ref[...])
    for s in range(SIGNALS):
        for h in range(2):
            out_ref[HALVES * h : HALVES * (h + 1), 0, PAIR * s : PAIR * (s + 1)] = spectra[ROWS * s : ROWS * (s + 1)]


def blocks_kernel(in_ref, there_ref, filter_there_ref, high_ref, low_ref, filter_high_ref, filter_low_ref, out_ref):
    half = lax.axis_index("ctx") // HALVES

    def spectra(table_ref, signals):
        cols = slice(PAIR * signals[0], PAIR * (signals[-1] + 1))
        high, low = split(jnp.concatenate([in_ref[n : n + 16, 0, cols] for n in range(0, BLOCKS, 16)], 0))
        terms = dot(table_ref[...], jnp.concatenate([high, high, low], 0))
        cosine, sine = terms[: 2 * BLOCKS], terms[2 * BLOCKS :]
        result = []
        for n in range(len(signals)):
            real, imag = slice(PAIR * n, PAIR * n + LANES), slice(PAIR * n + LANES, PAIR * (n + 1))
            result.append((cosine[:, real] + sine[:, imag], cosine[:, imag] - sine[:, real]))
        return result

    def blocks(table_high_ref, table_low_ref, values):
        cosine = jnp.concatenate([part for real, imag in values for part in (real, imag)], 1)
        sine = jnp.concatenate([part for real, imag in values for part in (-imag, real)], 1)
        high, low = split(jnp.concatenate([cosine, sine], 0))
        table_high = table_high_ref[half]
        both = dot(jnp.concatenate([table_high, table_low_ref[half]], 0), high)
        return both[:HALVES] + (dot(table_high, low) + both[HALVES:])

    ((taps_re, taps_im),) = spectra(filter_there_ref, [4])
    signals = spectra(there_ref, range(4))
    results, corr_re, corr_im = [], 0.0, 0.0
    for re, im in signals[:2]:
        results.append((taps_re * re - taps_im * im, taps_re * im + taps_im * re))
    for (mixed_re, mixed_im), (re, im) in zip(signals[:2], signals[2:]):
        results.append((taps_re * re + taps_im * im, taps_re * im - taps_im * re))
        corr_re += mixed_re * re + mixed_im * im
        corr_im += mixed_re * im - mixed_im * re
    out_ref[:, 0, : 4 * PAIR] = blocks(high_ref, low_ref, results)
    out_ref[:, 0, 4 * PAIR :] = blocks(filter_high_ref, filter_low_ref, [(corr_re, corr_im)])


def inverse_kernel(
    in_ref, query_ref, key_ref, values_ref, cot_ref, gain_ref, pair_ref, last_ref, twiddle_ref, high_ref, low_ref,
    out_ref, grad_query_ref, grad_key_ref, grad_values_ref, grad_filter_ref,
):
    f32, bf16 = jnp.float32, jnp.bfloat16
    spectra = jnp.concatenate([in_ref[:, 0, PAIR * s : PAIR * (s + 1)] for s in range(SIGNALS)], 0)
    spread = dot3(spectra, high_ref[...], low_ref[...])
    tw_re, tw_im = twiddle_ref[0], twiddle_ref[1]
    turned = []
    for s in range(SIGNALS):
        rows = slice(ROWS * s, ROWS * (s + 1))
        re, im = spread[rows, :LANES], spread[rows, LANES:]
        turned += [re * tw_re + im * tw_im, im * tw_re - re * tw_im]
    pairs = jnp.concatenate([jnp.concatenate(turned[:4], 0), jnp.concatenate(turned[4:8], 0)], 1)
    grad_filter = dot(last_ref[...], stack3(jnp.concatenate(turned[8:], 0)))
    for copy in range(grad_filter_ref.shape[0]):
        grad_filter_ref[copy] = grad_filter
    pairs = dot(pair_ref[...], stack3(pairs))
    query, cot = query_ref[...].astype(f32), cot_ref[...].astype(f32)
    key, value = key_ref[...].astype(f32), values_ref[...].astype(f32)
    first_channel = lax.broadcasted_iota(jnp.int32, query.shape, 0) % 2 == 0
    gain = jnp.where(first_channel, gain_ref[0], gain_ref[1])
    summed = pairs[:, :LANES] + gain * (key * value)
    out_ref[...] = (query * summed).astype(bf16)
    grad_query_ref[...] = (cot * summed).astype(bf16)
    grad_mixed = pairs[:, LANES:] + gain * (cot * query)
    grad_key_ref[...] = (grad_mixed * value).astype(bf16)
    grad_values_ref[...] = (grad_mixed * key).astype(bf16)


def finish_kernel(partials_ref, *refs):
    gated, outs, (total_ref, sems) = refs[:4], refs[4:9], refs[9:]
    copies = [pltpu.make_async_copy(src, dst, sems.at[n]) for n, (src, dst) in enumerate(zip((*gated, total_ref), outs))]
    for copy in copies[:4]:
        copy.start()
    total_ref[...] = jnp.sum(partials_ref[...], axis=0)
    copies[4].start()
    for copy in copies:
        copy.wait()


def by_rows(pair):
    return pair.reshape(2, ROWS, LANES).transpose(1, 0, 2).reshape(2 * ROWS, LANES)


def by_channel(rows):
    return rows.reshape(ROWS, 2, LANES).transpose(1, 0, 2).reshape(2, BLOCK)


def per_device(gate_q, gate_k, values, filter_taps, skip_gain, cotangent):
    f32 = jnp.float32
    first, last, twiddle, second, second_back = jax.tree.map(jnp.asarray, make_tables())
    groups = lax.axis_size("chan")
    gate_q, gate_k, values, cotangent = map(by_rows, (gate_q, gate_k, values, cotangent))
    vmem = pl.BlockSpec(memory_space=pltpu.VMEM)
    operands = (gate_k, values, cotangent, gate_q, filter_taps.reshape(ROWS, LANES), *first, twiddle, *second)
    sent = pl.pallas_call(
        forward_kernel,
        out_shape=jax.ShapeDtypeStruct((BLOCKS, 1, WIDTH), f32),
        in_specs=[pl.BlockSpec(memory_space=pltpu.HBM)] * len(operands),
        scratch_shapes=[
            *(pltpu.VMEM(v.shape, v.dtype) for v in operands),
            pltpu.SemaphoreType.DMA((len(operands),)),
        ],
        compiler_params=SMALL,
        name="forward_transform",
    )(*(pltpu.with_memory_space_constraint(v, pltpu.HBM) for v in operands))
    blocks = lax.all_to_all(sent, "ctx", 0, 0, tiled=True, axis_index_groups=CTX_ORDER)
    sent = pl.pallas_call(
        blocks_kernel,
        out_shape=jax.ShapeDtypeStruct((HALVES, 1, WIDTH), f32),
        compiler_params=SMALL,
        name="block_convolutions",
    )(blocks, *jax.tree.map(jnp.asarray, make_block_tables()))
    spectra = lax.all_to_all(sent, "ctx", 0, 0, tiled=True, axis_index_groups=HALF_ORDER)
    like = pltpu.VMEM(gate_q.shape, jnp.bfloat16)
    *gated, partial_filter = pl.pallas_call(
        inverse_kernel,
        out_shape=(like, like, like, like, jax.ShapeDtypeStruct((groups, ROWS, LANES), f32)),
        in_specs=[vmem] * 5 + [pl.BlockSpec(memory_space=pltpu.SMEM)] + [vmem] * 5,
        compiler_params=SMALL,
        name="inverse_transform",
    )(spectra, gate_q, gate_k, values, cotangent, skip_gain, *last, twiddle, *second_back)
    partials = lax.all_to_all(partial_filter, "chan", 0, 0, tiled=True, axis_index_groups=CHAN_ORDER)
    like = jax.ShapeDtypeStruct(gate_q.shape, jnp.bfloat16)
    *gated, grad_filter = pl.pallas_call(
        finish_kernel,
        out_shape=(like, like, like, like, jax.ShapeDtypeStruct((ROWS, LANES), f32)),
        out_specs=[pl.BlockSpec(memory_space=pltpu.HBM)] * 5,
        scratch_shapes=[pltpu.VMEM((ROWS, LANES), f32), pltpu.SemaphoreType.DMA((5,))],
        compiler_params=SMALL,
        name="finish",
    )(partials, *gated)
    return (*map(by_channel, gated), grad_filter.reshape(BLOCK))


def solution(mesh):
    return jax.shard_map(
        per_device,
        mesh=mesh,
        in_specs=(
            P("chan", "ctx"),
            P("chan", "ctx"),
            P("chan", "ctx"),
            P("ctx"),
            P("chan"),
            P("chan", "ctx"),
        ),
        out_specs=(
            P("chan", "ctx"),
            P("chan", "ctx"),
            P("chan", "ctx"),
            P("chan", "ctx"),
            P("ctx"),
        ),
        check_vma=False,
    )
```

```python
import numpy as np

import jax
import jax.numpy as jnp
from jax import lax
from jax.experimental import pallas as pl
from jax.experimental.pallas import tpu as pltpu
from jax.sharding import PartitionSpec as P

BLOCK = 4096
BLOCKS = 64
ROWS = 32
LANES = 128
HALVES = 32
SIGNALS = 5
PAIR = 2 * LANES
WIDTH = SIGNALS * PAIR
SMALL = pltpu.CompilerParams(vmem_limit_bytes=8 << 20)
CORNER = 20
PLANE_ORDER = [CORNER if p == 0 else 0 if p == CORNER else p for p in range(HALVES)]
CTX_ORDER = [[HALVES + p for p in PLANE_ORDER] + PLANE_ORDER]
HALF_ORDER = [PLANE_ORDER, [HALVES + p for p in PLANE_ORDER]]
CHAN_ORDER = [[5, 4, 2, 3, 6, 7, 0, 1]]


def split(value):
    high = value.astype(jnp.bfloat16)
    return high, (value - high.astype(jnp.float32)).astype(jnp.bfloat16)


def split_table(table):
    high = table.astype(np.float32).astype(jnp.bfloat16)
    low = (table - high.astype(np.float64)).astype(np.float32).astype(jnp.bfloat16)
    return high, low


def make_tables():
    a = np.arange(ROWS)
    b = np.arange(LANES)
    first = np.exp(-2j * np.pi * (a[:, None] * a[None, :] / ROWS + LANES * a[None, :] / (4 * BLOCK)))
    first = np.concatenate([first.real, first.imag], 0)
    first_pair = np.zeros((2, 2 * ROWS, ROWS, 2))
    first_pair[0, :, :, 0] = first_pair[1, :, :, 1] = first
    last = np.exp(2j * np.pi * (a[:, None] * a[None, :] / ROWS + LANES * a[:, None] / (4 * BLOCK)))
    last = np.concatenate([last.real, -last.imag], 1) / BLOCK / (BLOCK * BLOCKS) ** 0.5
    last_pair = np.zeros((ROWS, 2, 2, 2 * ROWS))
    last_pair[:, 0, 0] = last_pair[:, 1, 1] = last

    def thrice(table):
        high, low = split_table(table)
        return np.concatenate([high, low, high], 1)

    first_table = thrice(first_pair.reshape(4 * ROWS, 2 * ROWS)), thrice(first)
    last_table = thrice(last_pair.reshape(2 * ROWS, 4 * ROWS)), thrice(last)
    twiddle = np.exp(-2j * np.pi * b[None, :] * (4 * a[:, None] + 1) / (4 * BLOCK))
    twiddle = np.stack([twiddle.real, twiddle.imag]).astype(np.float32)
    angle = 2 * np.pi * (b[:, None] * b[None, :] % LANES) / LANES
    cos, sin = np.cos(angle), np.sin(angle)
    second = np.block([[cos, -sin], [sin, cos]])
    return first_table, last_table, twiddle, split_table(second), split_table(second.T)


def make_block_tables():
    blocks = np.array(CTX_ORDER[0])
    phases = np.arange(2 * BLOCKS)
    wave = np.exp(-2j * np.pi * phases[:, None] * blocks[None, :] / (2 * BLOCKS))
    step = np.exp(-2j * np.pi * phases / (2 * BLOCKS))
    back = np.conj(wave.T) / (2 * BLOCKS)

    def there(table):
        high, low = split_table(np.concatenate([table.real, -table.imag], 0))
        return np.concatenate([high, low, high], 1)

    def here(table):
        rows = [table[HALVES:], table[:HALVES]]
        return split_table(np.stack([np.concatenate([t.real, t.imag], 1) for t in rows]))

    filter_wave = wave * (1 + 1j * step)[:, None]
    filter_back = back * (1 - 1j * np.conj(step))[None, :]
    return there(wave), there(filter_wave), *here(back), *here(filter_back)


def dot(left, right):
    return jnp.dot(left, right, preferred_element_type=jnp.float32)


def dot3(value, high, low):
    value_high, value_low = split(value)
    rows = value.shape[0]
    both = dot(jnp.concatenate([value_high, value_low], 0), high)
    return both[:rows] + (dot(value_high, low) + both[rows:])


def stack3(value):
    high, low = split(value)
    return jnp.concatenate([high, high, low], 0)


def forward_kernel(*refs):
    operands, (out_ref, gain_ref, *held, sems) = refs[:11], refs[11:]
    copies = [pltpu.make_async_copy(src, dst, sems.at[n]) for n, (src, dst) in enumerate(zip(operands, held))]
    for copy in copies:
        copy.start()
    key_ref, values_ref, cot_ref, query_ref, taps_ref, pair_ref, first_ref, twiddle_ref, high_ref, low_ref, skip_ref = held
    f32 = jnp.float32
    for copy in copies[:5]:
        copy.wait()
    mixed = key_ref[...].astype(f32) * values_ref[...].astype(f32)
    grad = cot_ref[...].astype(f32) * query_ref[...].astype(f32)
    pairs, taps = stack3(jnp.concatenate([mixed, grad], 1)), stack3(taps_ref[...])
    for copy in copies[5:7]:
        copy.wait()
    pairs, taps = dot(pair_ref[...], pairs), dot(first_ref[...], taps)
    copies[7].wait()
    tw_re, tw_im = twiddle_ref[0], twiddle_ref[1]
    places = [(pairs, 0, 0), (pairs, 1, 0), (pairs, 0, 1), (pairs, 1, 1), (taps, 0, 0)]
    turned = []
    for spread, row, col in places:
        cols = slice(LANES * col, LANES * (col + 1))
        re = spread[2 * ROWS * row : 2 * ROWS * row + ROWS, cols]
        im = spread[2 * ROWS * row + ROWS : 2 * ROWS * (row + 1), cols]
        turned.append(jnp.concatenate([re * tw_re - im * tw_im, re * tw_im + im * tw_re], 1))
    for copy in copies[8:]:
        copy.wait()
    spectra = dot3(jnp.concatenate(turned, 0), high_ref[...], low_ref[...])
    for s in range(SIGNALS):
        for h in range(2):
            out_ref[HALVES * h : HALVES * (h + 1), 0, PAIR * s : PAIR * (s + 1)] = spectra[ROWS * s : ROWS * (s + 1)]
    first_channel = lax.broadcasted_iota(jnp.int32, gain_ref.shape, 0) % 2 == 0
    gain_ref[...] = jnp.where(first_channel, skip_ref[:, 0:1], skip_ref[:, 1:2])


def blocks_kernel(in_ref, there_ref, filter_there_ref, high_ref, low_ref, filter_high_ref, filter_low_ref, out_ref):
    half = lax.axis_index("ctx") // HALVES

    def spectra(table_ref, signals):
        cols = slice(PAIR * signals[0], PAIR * (signals[-1] + 1))
        high, low = split(jnp.concatenate([in_ref[n : n + 16, 0, cols] for n in range(0, BLOCKS, 16)], 0))
        terms = dot(table_ref[...], jnp.concatenate([high, high, low], 0))
        cosine, sine = terms[: 2 * BLOCKS], terms[2 * BLOCKS :]
        result = []
        for n in range(len(signals)):
            real, imag = slice(PAIR * n, PAIR * n + LANES), slice(PAIR * n + LANES, PAIR * (n + 1))
            result.append((cosine[:, real] + sine[:, imag], cosine[:, imag] - sine[:, real]))
        return result

    def blocks(table_high_ref, table_low_ref, values):
        cosine = jnp.concatenate([part for real, imag in values for part in (real, imag)], 1)
        sine = jnp.concatenate([part for real, imag in values for part in (-imag, real)], 1)
        high, low = split(jnp.concatenate([cosine, sine], 0))
        table_high = table_high_ref[half]
        both = dot(jnp.concatenate([table_high, table_low_ref[half]], 0), high)
        return both[:HALVES] + (dot(table_high, low) + both[HALVES:])

    ((taps_re, taps_im),) = spectra(filter_there_ref, [4])
    signals = spectra(there_ref, range(4))
    results, corr_re, corr_im = [], 0.0, 0.0
    for re, im in signals[:2]:
        results.append((taps_re * re - taps_im * im, taps_re * im + taps_im * re))
    for (mixed_re, mixed_im), (re, im) in zip(signals[:2], signals[2:]):
        results.append((taps_re * re + taps_im * im, taps_re * im - taps_im * re))
        corr_re += mixed_re * re + mixed_im * im
        corr_im += mixed_re * im - mixed_im * re
    out_ref[:, 0, : 4 * PAIR] = blocks(high_ref, low_ref, results)
    out_ref[:, 0, 4 * PAIR :] = blocks(filter_high_ref, filter_low_ref, [(corr_re, corr_im)])


def inverse_kernel(
    in_ref, query_ref, key_ref, values_ref, cot_ref, gain_ref, pair_ref, last_ref, twiddle_ref, high_ref, low_ref,
    out_ref, grad_query_ref, grad_key_ref, grad_values_ref, grad_filter_ref,
):
    f32, bf16 = jnp.float32, jnp.bfloat16
    spectra = jnp.concatenate([in_ref[:, 0, PAIR * s : PAIR * (s + 1)] for s in range(SIGNALS)], 0)
    spread = dot3(spectra, high_ref[...], low_ref[...])
    tw_re, tw_im = twiddle_ref[0], twiddle_ref[1]
    turned = []
    for s in range(SIGNALS):
        rows = slice(ROWS * s, ROWS * (s + 1))
        re, im = spread[rows, :LANES], spread[rows, LANES:]
        turned += [re * tw_re + im * tw_im, im * tw_re - re * tw_im]
    pairs = jnp.concatenate([jnp.concatenate(turned[:4], 0), jnp.concatenate(turned[4:8], 0)], 1)
    grad_filter = dot(last_ref[...], stack3(jnp.concatenate(turned[8:], 0)))
    for copy in range(grad_filter_ref.shape[0]):
        grad_filter_ref[copy] = grad_filter
    pairs = dot(pair_ref[...], stack3(pairs))
    query, cot = query_ref[...].astype(f32), cot_ref[...].astype(f32)
    key, value = key_ref[...].astype(f32), values_ref[...].astype(f32)
    gain = gain_ref[...]
    summed = pairs[:, :LANES] + gain * (key * value)
    out_ref[...] = (query * summed).astype(bf16)
    grad_query_ref[...] = (cot * summed).astype(bf16)
    grad_mixed = pairs[:, LANES:] + gain * (cot * query)
    grad_key_ref[...] = (grad_mixed * value).astype(bf16)
    grad_values_ref[...] = (grad_mixed * key).astype(bf16)


def finish_kernel(partials_ref, *refs):
    gated, outs, (total_ref, sems) = refs[:4], refs[4:9], refs[9:]
    copies = [pltpu.make_async_copy(src, dst, sems.at[n]) for n, (src, dst) in enumerate(zip((*gated, total_ref), outs))]
    for copy in copies[:4]:
        copy.start()
    total_ref[...] = jnp.sum(partials_ref[...], axis=0)
    copies[4].start()
    for copy in copies:
        copy.wait()


def by_rows(pair):
    return pair.reshape(2, ROWS, LANES).transpose(1, 0, 2).reshape(2 * ROWS, LANES)


def by_channel(rows):
    return rows.reshape(ROWS, 2, LANES).transpose(1, 0, 2).reshape(2, BLOCK)


def per_device(gate_q, gate_k, values, filter_taps, skip_gain, cotangent):
    f32 = jnp.float32
    first, last, twiddle, second, second_back = jax.tree.map(jnp.asarray, make_tables())
    groups = lax.axis_size("chan")
    gate_q, gate_k, values, cotangent = map(by_rows, (gate_q, gate_k, values, cotangent))
    operands = (gate_k, values, cotangent, gate_q, filter_taps.reshape(ROWS, LANES), *first, twiddle, *second, skip_gain[None])
    sent, gain = pl.pallas_call(
        forward_kernel,
        out_shape=(jax.ShapeDtypeStruct((BLOCKS, 1, WIDTH), f32), pltpu.VMEM(gate_q.shape, f32)),
        in_specs=[pl.BlockSpec(memory_space=pltpu.HBM)] * len(operands),
        scratch_shapes=[
            *(pltpu.VMEM(v.shape, v.dtype) for v in operands),
            pltpu.SemaphoreType.DMA((len(operands),)),
        ],
        compiler_params=SMALL,
        name="forward_transform",
    )(*(pltpu.with_memory_space_constraint(v, pltpu.HBM) for v in operands))
    blocks = lax.all_to_all(sent, "ctx", 0, 0, tiled=True, axis_index_groups=CTX_ORDER)
    sent = pl.pallas_call(
        blocks_kernel,
        out_shape=jax.ShapeDtypeStruct((HALVES, 1, WIDTH), f32),
        compiler_params=SMALL,
        name="block_convolutions",
    )(blocks, *jax.tree.map(jnp.asarray, make_block_tables()))
    spectra = lax.all_to_all(sent, "ctx", 0, 0, tiled=True, axis_index_groups=HALF_ORDER)
    like = pltpu.VMEM(gate_q.shape, jnp.bfloat16)
    *gated, partial_filter = pl.pallas_call(
        inverse_kernel,
        out_shape=(like, like, like, like, jax.ShapeDtypeStruct((groups, ROWS, LANES), f32)),
        compiler_params=SMALL,
        name="inverse_transform",
    )(spectra, gate_q, gate_k, values, cotangent, gain, *last, twiddle, *second_back)
    partials = lax.all_to_all(partial_filter, "chan", 0, 0, tiled=True, axis_index_groups=CHAN_ORDER)
    like = jax.ShapeDtypeStruct(gate_q.shape, jnp.bfloat16)
    *gated, grad_filter = pl.pallas_call(
        finish_kernel,
        out_shape=(like, like, like, like, jax.ShapeDtypeStruct((ROWS, LANES), f32)),
        out_specs=[pl.BlockSpec(memory_space=pltpu.HBM)] * 5,
        scratch_shapes=[pltpu.VMEM((ROWS, LANES), f32), pltpu.SemaphoreType.DMA((5,))],
        compiler_params=SMALL,
        name="finish",
    )(partials, *gated)
    return (*map(by_channel, gated), grad_filter.reshape(BLOCK))


def solution(mesh):
    return jax.shard_map(
        per_device,
        mesh=mesh,
        in_specs=(
            P("chan", "ctx"),
            P("chan", "ctx"),
            P("chan", "ctx"),
            P("ctx"),
            P("chan"),
            P("chan", "ctx"),
        ),
        out_specs=(
            P("chan", "ctx"),
            P("chan", "ctx"),
            P("chan", "ctx"),
            P("chan", "ctx"),
            P("ctx"),
        ),
        check_vma=False,
    )
```

```python
import numpy as np

import jax
import jax.numpy as jnp
from jax import lax
from jax.experimental import pallas as pl
from jax.experimental.pallas import tpu as pltpu
from jax.sharding import PartitionSpec as P

BLOCK = 4096
BLOCKS = 64
ROWS = 32
LANES = 128
HALVES = 32
SIGNALS = 5
PAIR = 2 * LANES
WIDTH = SIGNALS * PAIR
SMALL = pltpu.CompilerParams(vmem_limit_bytes=8 << 20)
def plane_order(corner):
    return [corner if p == 0 else 0 if p == corner else p for p in range(HALVES)]


FIRST_ORDER, SECOND_ORDER = plane_order(21), plane_order(20)
CTX_ORDER = [[HALVES + p for p in FIRST_ORDER] + FIRST_ORDER]
HALF_ORDER = [SECOND_ORDER, [HALVES + p for p in SECOND_ORDER]]
CHAN_ORDER = [[5, 4, 2, 3, 6, 7, 0, 1]]


def split(value):
    high = value.astype(jnp.bfloat16)
    return high, (value - high.astype(jnp.float32)).astype(jnp.bfloat16)


def split_table(table):
    high = table.astype(np.float32).astype(jnp.bfloat16)
    low = (table - high.astype(np.float64)).astype(np.float32).astype(jnp.bfloat16)
    return high, low


def make_tables():
    a = np.arange(ROWS)
    b = np.arange(LANES)
    first = np.exp(-2j * np.pi * (a[:, None] * a[None, :] / ROWS + LANES * a[None, :] / (4 * BLOCK)))
    first = np.concatenate([first.real, first.imag], 0)
    first_pair = np.zeros((2, 2 * ROWS, ROWS, 2))
    first_pair[0, :, :, 0] = first_pair[1, :, :, 1] = first
    k1 = np.array([FIRST_ORDER.index(p) for p in SECOND_ORDER])
    last = np.exp(2j * np.pi * (a[:, None] * k1[None, :] / ROWS + LANES * a[:, None] / (4 * BLOCK)))
    last = np.concatenate([last.real, -last.imag], 1) / BLOCK / (BLOCK * BLOCKS) ** 0.5
    last_pair = np.zeros((ROWS, 2, 2, 2 * ROWS))
    last_pair[:, 0, 0] = last_pair[:, 1, 1] = last

    def thrice(table):
        high, low = split_table(table)
        return np.concatenate([high, low, high], 1)

    first_table = thrice(first_pair.reshape(4 * ROWS, 2 * ROWS)), thrice(first)
    last_table = thrice(last_pair.reshape(2 * ROWS, 4 * ROWS)), thrice(last)
    twiddle = np.exp(-2j * np.pi * b[None, :] * (4 * a[:, None] + 1) / (4 * BLOCK))
    twiddle = np.stack([twiddle.real, twiddle.imag]).astype(np.float32)
    twiddle = twiddle, twiddle[:, k1]
    angle = 2 * np.pi * (b[:, None] * b[None, :] % LANES) / LANES
    cos, sin = np.cos(angle), np.sin(angle)
    second = np.block([[cos, -sin], [sin, cos]])
    return first_table, last_table, twiddle, split_table(second), split_table(second.T)


def make_block_tables():
    blocks = np.array(CTX_ORDER[0])
    results = np.array(HALF_ORDER)
    phases = np.arange(2 * BLOCKS)
    wave = np.exp(-2j * np.pi * phases[:, None] * blocks[None, :] / (2 * BLOCKS))
    step = np.exp(-2j * np.pi * phases / (2 * BLOCKS))
    back = np.exp(2j * np.pi * results[:, :, None] * phases / (2 * BLOCKS)) / (2 * BLOCKS)

    def there(table):
        high, low = split_table(np.concatenate([table.real, -table.imag], 0))
        return np.concatenate([high, low, high], 1)

    def here(table):
        return split_table(np.concatenate([table.real, table.imag], 2))

    filter_wave = wave * (1 + 1j * step)[:, None]
    filter_back = back * (1 - 1j * np.conj(step))
    return there(wave), there(filter_wave), *here(back), *here(filter_back)


def dot(left, right):
    return jnp.dot(left, right, preferred_element_type=jnp.float32)


def dot3(value, high, low):
    value_high, value_low = split(value)
    rows = value.shape[0]
    both = dot(jnp.concatenate([value_high, value_low], 0), high)
    return both[:rows] + (dot(value_high, low) + both[rows:])


def stack3(value):
    high, low = split(value)
    return jnp.concatenate([high, high, low], 0)


def forward_kernel(*refs):
    operands, (out_ref, gain_ref, *held, sems) = refs[:11], refs[11:]
    copies = [pltpu.make_async_copy(src, dst, sems.at[n]) for n, (src, dst) in enumerate(zip(operands, held))]
    for copy in copies:
        copy.start()
    key_ref, values_ref, cot_ref, query_ref, taps_ref, pair_ref, first_ref, twiddle_ref, high_ref, low_ref, skip_ref = held
    f32 = jnp.float32
    for copy in copies[:5]:
        copy.wait()
    mixed = key_ref[...].astype(f32) * values_ref[...].astype(f32)
    grad = cot_ref[...].astype(f32) * query_ref[...].astype(f32)
    pairs, taps = stack3(jnp.concatenate([mixed, grad], 1)), stack3(taps_ref[...])
    for copy in copies[5:7]:
        copy.wait()
    pairs, taps = dot(pair_ref[...], pairs), dot(first_ref[...], taps)
    copies[7].wait()
    tw_re, tw_im = twiddle_ref[0], twiddle_ref[1]
    places = [(pairs, 0, 0), (pairs, 1, 0), (pairs, 0, 1), (pairs, 1, 1), (taps, 0, 0)]
    turned = []
    for spread, row, col in places:
        cols = slice(LANES * col, LANES * (col + 1))
        re = spread[2 * ROWS * row : 2 * ROWS * row + ROWS, cols]
        im = spread[2 * ROWS * row + ROWS : 2 * ROWS * (row + 1), cols]
        turned.append(jnp.concatenate([re * tw_re - im * tw_im, re * tw_im + im * tw_re], 1))
    for copy in copies[8:]:
        copy.wait()
    spectra = dot3(jnp.concatenate(turned, 0), high_ref[...], low_ref[...])
    for s in range(SIGNALS):
        for h in range(2):
            out_ref[HALVES * h : HALVES * (h + 1), 0, PAIR * s : PAIR * (s + 1)] = spectra[ROWS * s : ROWS * (s + 1)]
    first_channel = lax.broadcasted_iota(jnp.int32, gain_ref.shape, 0) % 2 == 0
    gain_ref[...] = jnp.where(first_channel, skip_ref[:, 0:1], skip_ref[:, 1:2])


def blocks_kernel(in_ref, there_ref, filter_there_ref, high_ref, low_ref, filter_high_ref, filter_low_ref, out_ref):
    half = lax.axis_index("ctx") // HALVES

    def spectra(table_ref, signals):
        cols = slice(PAIR * signals[0], PAIR * (signals[-1] + 1))
        high, low = split(jnp.concatenate([in_ref[n : n + 16, 0, cols] for n in range(0, BLOCKS, 16)], 0))
        terms = dot(table_ref[...], jnp.concatenate([high, high, low], 0))
        cosine, sine = terms[: 2 * BLOCKS], terms[2 * BLOCKS :]
        result = []
        for n in range(len(signals)):
            real, imag = slice(PAIR * n, PAIR * n + LANES), slice(PAIR * n + LANES, PAIR * (n + 1))
            result.append((cosine[:, real] + sine[:, imag], cosine[:, imag] - sine[:, real]))
        return result

    def blocks(table_high_ref, table_low_ref, values):
        cosine = jnp.concatenate([part for real, imag in values for part in (real, imag)], 1)
        sine = jnp.concatenate([part for real, imag in values for part in (-imag, real)], 1)
        high, low = split(jnp.concatenate([cosine, sine], 0))
        table_high = table_high_ref[half]
        both = dot(jnp.concatenate([table_high, table_low_ref[half]], 0), high)
        return both[:HALVES] + (dot(table_high, low) + both[HALVES:])

    ((taps_re, taps_im),) = spectra(filter_there_ref, [4])
    signals = spectra(there_ref, range(4))
    results, corr_re, corr_im = [], 0.0, 0.0
    for re, im in signals[:2]:
        results.append((taps_re * re - taps_im * im, taps_re * im + taps_im * re))
    for (mixed_re, mixed_im), (re, im) in zip(signals[:2], signals[2:]):
        results.append((taps_re * re + taps_im * im, taps_re * im - taps_im * re))
        corr_re += mixed_re * re + mixed_im * im
        corr_im += mixed_re * im - mixed_im * re
    out_ref[:, 0, : 4 * PAIR] = blocks(high_ref, low_ref, results)
    out_ref[:, 0, 4 * PAIR :] = blocks(filter_high_ref, filter_low_ref, [(corr_re, corr_im)])


def inverse_kernel(
    in_ref, query_ref, key_ref, values_ref, cot_ref, gain_ref, pair_ref, last_ref, twiddle_ref, high_ref, low_ref,
    out_ref, grad_query_ref, grad_key_ref, grad_values_ref, grad_filter_ref,
):
    f32, bf16 = jnp.float32, jnp.bfloat16
    spectra = jnp.concatenate([in_ref[:, 0, PAIR * s : PAIR * (s + 1)] for s in range(SIGNALS)], 0)
    spread = dot3(spectra, high_ref[...], low_ref[...])
    tw_re, tw_im = twiddle_ref[0], twiddle_ref[1]
    turned = []
    for s in range(SIGNALS):
        rows = slice(ROWS * s, ROWS * (s + 1))
        re, im = spread[rows, :LANES], spread[rows, LANES:]
        turned += [re * tw_re + im * tw_im, im * tw_re - re * tw_im]
    pairs = jnp.concatenate([jnp.concatenate(turned[:4], 0), jnp.concatenate(turned[4:8], 0)], 1)
    grad_filter = dot(last_ref[...], stack3(jnp.concatenate(turned[8:], 0)))
    for copy in range(grad_filter_ref.shape[0]):
        grad_filter_ref[copy] = grad_filter
    pairs = dot(pair_ref[...], stack3(pairs))
    query, cot = query_ref[...].astype(f32), cot_ref[...].astype(f32)
    key, value = key_ref[...].astype(f32), values_ref[...].astype(f32)
    gain = gain_ref[...]
    summed = pairs[:, :LANES] + gain * (key * value)
    out_ref[...] = (query * summed).astype(bf16)
    grad_query_ref[...] = (cot * summed).astype(bf16)
    grad_mixed = pairs[:, LANES:] + gain * (cot * query)
    grad_key_ref[...] = (grad_mixed * value).astype(bf16)
    grad_values_ref[...] = (grad_mixed * key).astype(bf16)


def finish_kernel(partials_ref, *refs):
    gated, outs, (total_ref, sems) = refs[:4], refs[4:9], refs[9:]
    copies = [pltpu.make_async_copy(src, dst, sems.at[n]) for n, (src, dst) in enumerate(zip((*gated, total_ref), outs))]
    for copy in copies[:4]:
        copy.start()
    total_ref[...] = jnp.sum(partials_ref[...], axis=0)
    copies[4].start()
    for copy in copies:
        copy.wait()


def by_rows(pair):
    return pair.reshape(2, ROWS, LANES).transpose(1, 0, 2).reshape(2 * ROWS, LANES)


def by_channel(rows):
    return rows.reshape(ROWS, 2, LANES).transpose(1, 0, 2).reshape(2, BLOCK)


def per_device(gate_q, gate_k, values, filter_taps, skip_gain, cotangent):
    f32 = jnp.float32
    first, last, twiddle, second, second_back = jax.tree.map(jnp.asarray, make_tables())
    groups = lax.axis_size("chan")
    gate_q, gate_k, values, cotangent = map(by_rows, (gate_q, gate_k, values, cotangent))
    operands = (gate_k, values, cotangent, gate_q, filter_taps.reshape(ROWS, LANES), *first, twiddle[0], *second, skip_gain[None])
    sent, gain = pl.pallas_call(
        forward_kernel,
        out_shape=(jax.ShapeDtypeStruct((BLOCKS, 1, WIDTH), f32), pltpu.VMEM(gate_q.shape, f32)),
        in_specs=[pl.BlockSpec(memory_space=pltpu.HBM)] * len(operands),
        scratch_shapes=[
            *(pltpu.VMEM(v.shape, v.dtype) for v in operands),
            pltpu.SemaphoreType.DMA((len(operands),)),
        ],
        compiler_params=SMALL,
        name="forward_transform",
    )(*(pltpu.with_memory_space_constraint(v, pltpu.HBM) for v in operands))
    blocks = lax.all_to_all(sent, "ctx", 0, 0, tiled=True, axis_index_groups=CTX_ORDER)
    sent = pl.pallas_call(
        blocks_kernel,
        out_shape=jax.ShapeDtypeStruct((HALVES, 1, WIDTH), f32),
        compiler_params=SMALL,
        name="block_convolutions",
    )(blocks, *jax.tree.map(jnp.asarray, make_block_tables()))
    spectra = lax.all_to_all(sent, "ctx", 0, 0, tiled=True, axis_index_groups=HALF_ORDER)
    like = pltpu.VMEM(gate_q.shape, jnp.bfloat16)
    *gated, partial_filter = pl.pallas_call(
        inverse_kernel,
        out_shape=(like, like, like, like, jax.ShapeDtypeStruct((groups, ROWS, LANES), f32)),
        compiler_params=SMALL,
        name="inverse_transform",
    )(spectra, gate_q, gate_k, values, cotangent, gain, *last, twiddle[1], *second_back)
    partials = lax.all_to_all(partial_filter, "chan", 0, 0, tiled=True, axis_index_groups=CHAN_ORDER)
    like = jax.ShapeDtypeStruct(gate_q.shape, jnp.bfloat16)
    *gated, grad_filter = pl.pallas_call(
        finish_kernel,
        out_shape=(like, like, like, like, jax.ShapeDtypeStruct((ROWS, LANES), f32)),
        out_specs=[pl.BlockSpec(memory_space=pltpu.HBM)] * 5,
        scratch_shapes=[pltpu.VMEM((ROWS, LANES), f32), pltpu.SemaphoreType.DMA((5,))],
        compiler_params=SMALL,
        name="finish",
    )(partials, *gated)
    return (*map(by_channel, gated), grad_filter.reshape(BLOCK))


def solution(mesh):
    return jax.shard_map(
        per_device,
        mesh=mesh,
        in_specs=(
            P("chan", "ctx"),
            P("chan", "ctx"),
            P("chan", "ctx"),
            P("ctx"),
            P("chan"),
            P("chan", "ctx"),
        ),
        out_specs=(
            P("chan", "ctx"),
            P("chan", "ctx"),
            P("chan", "ctx"),
            P("chan", "ctx"),
            P("ctx"),
        ),
        check_vma=False,
    )
```

```python
import numpy as np

import jax
import jax.numpy as jnp
from jax import lax
from jax.experimental import pallas as pl
from jax.experimental.pallas import tpu as pltpu
from jax.sharding import PartitionSpec as P

BLOCK = 4096
BLOCKS = 64
ROWS = 32
LANES = 128
HALVES = 32
SIGNALS = 5
PAIR = 2 * LANES
WIDTH = SIGNALS * PAIR
SMALL = pltpu.CompilerParams(vmem_limit_bytes=8 << 20)
def plane_order(corner):
    return [corner if p == 0 else 0 if p == corner else p for p in range(HALVES)]


FIRST_ORDER, SECOND_ORDER = plane_order(22), plane_order(20)
CTX_ORDER = [[HALVES + p for p in FIRST_ORDER] + FIRST_ORDER]
HALF_ORDER = [SECOND_ORDER, [HALVES + p for p in SECOND_ORDER]]
CHAN_ORDER = [[5, 4, 2, 3, 6, 7, 0, 1]]


def split(value):
    high = value.astype(jnp.bfloat16)
    return high, (value - high.astype(jnp.float32)).astype(jnp.bfloat16)


def split_table(table):
    high = table.astype(np.float32).astype(jnp.bfloat16)
    low = (table - high.astype(np.float64)).astype(np.float32).astype(jnp.bfloat16)
    return high, low


def make_tables():
    a = np.arange(ROWS)
    b = np.arange(LANES)
    first = np.exp(-2j * np.pi * (a[:, None] * a[None, :] / ROWS + LANES * a[None, :] / (4 * BLOCK)))
    first = np.concatenate([first.real, first.imag], 0)
    first_pair = np.zeros((2, 2 * ROWS, ROWS, 2))
    first_pair[0, :, :, 0] = first_pair[1, :, :, 1] = first
    k1 = np.array([FIRST_ORDER.index(p) for p in SECOND_ORDER])
    last = np.exp(2j * np.pi * (a[:, None] * k1[None, :] / ROWS + LANES * a[:, None] / (4 * BLOCK)))
    last = np.concatenate([last.real, -last.imag], 1) / BLOCK / (BLOCK * BLOCKS) ** 0.5
    last_pair = np.zeros((ROWS, 2, 2, 2 * ROWS))
    last_pair[:, 0, 0] = last_pair[:, 1, 1] = last

    def thrice(table):
        high, low = split_table(table)
        return np.concatenate([high, low, high], 1)

    first_table = thrice(first_pair.reshape(4 * ROWS, 2 * ROWS)), thrice(first)
    last_table = thrice(last_pair.reshape(2 * ROWS, 4 * ROWS)), thrice(last)
    twiddle = np.exp(-2j * np.pi * b[None, :] * (4 * a[:, None] + 1) / (4 * BLOCK))
    twiddle = np.stack([twiddle.real, twiddle.imag]).astype(np.float32)
    twiddle = twiddle, twiddle[:, k1]
    angle = 2 * np.pi * (b[:, None] * b[None, :] % LANES) / LANES
    cos, sin = np.cos(angle), np.sin(angle)
    second = np.block([[cos, -sin], [sin, cos]])
    return first_table, last_table, twiddle, split_table(second), split_table(second.T)


def make_block_tables():
    blocks = np.array(CTX_ORDER[0])
    results = np.array(HALF_ORDER)
    phases = np.arange(2 * BLOCKS)
    wave = np.exp(-2j * np.pi * phases[:, None] * blocks[None, :] / (2 * BLOCKS))
    step = np.exp(-2j * np.pi * phases / (2 * BLOCKS))
    back = np.exp(2j * np.pi * results[:, :, None] * phases / (2 * BLOCKS)) / (2 * BLOCKS)

    def there(table):
        high, low = split_table(np.concatenate([table.real, -table.imag], 0))
        return np.concatenate([high, low, high], 1)

    def here(table):
        return split_table(np.concatenate([table.real, table.imag], 2))

    filter_wave = wave * (1 + 1j * step)[:, None]
    filter_back = back * (1 - 1j * np.conj(step))
    return there(wave), there(filter_wave), *here(back), *here(filter_back)


def dot(left, right):
    return jnp.dot(left, right, preferred_element_type=jnp.float32)


def dot3(value, high, low):
    value_high, value_low = split(value)
    rows = value.shape[0]
    both = dot(jnp.concatenate([value_high, value_low], 0), high)
    return both[:rows] + (dot(value_high, low) + both[rows:])


def stack3(value):
    high, low = split(value)
    return jnp.concatenate([high, high, low], 0)


def forward_kernel(*refs):
    operands, (out_ref, gain_ref, *held, sems) = refs[:11], refs[11:]
    copies = [pltpu.make_async_copy(src, dst, sems.at[n]) for n, (src, dst) in enumerate(zip(operands, held))]
    for copy in copies:
        copy.start()
    key_ref, values_ref, cot_ref, query_ref, taps_ref, pair_ref, first_ref, twiddle_ref, high_ref, low_ref, skip_ref = held
    f32 = jnp.float32
    for copy in copies[:5]:
        copy.wait()
    mixed = key_ref[...].astype(f32) * values_ref[...].astype(f32)
    grad = cot_ref[...].astype(f32) * query_ref[...].astype(f32)
    pairs, taps = stack3(jnp.concatenate([mixed, grad], 1)), stack3(taps_ref[...])
    for copy in copies[5:7]:
        copy.wait()
    pairs, taps = dot(pair_ref[...], pairs), dot(first_ref[...], taps)
    copies[7].wait()
    tw_re, tw_im = twiddle_ref[0], twiddle_ref[1]
    places = [(pairs, 0, 0), (pairs, 1, 0), (pairs, 0, 1), (pairs, 1, 1), (taps, 0, 0)]
    turned = []
    for spread, row, col in places:
        cols = slice(LANES * col, LANES * (col + 1))
        re = spread[2 * ROWS * row : 2 * ROWS * row + ROWS, cols]
        im = spread[2 * ROWS * row + ROWS : 2 * ROWS * (row + 1), cols]
        turned.append(jnp.concatenate([re * tw_re - im * tw_im, re * tw_im + im * tw_re], 1))
    for copy in copies[8:]:
        copy.wait()
    spectra = dot3(jnp.concatenate(turned, 0), high_ref[...], low_ref[...])
    for s in range(SIGNALS):
        for h in range(2):
            out_ref[HALVES * h : HALVES * (h + 1), 0, PAIR * s : PAIR * (s + 1)] = spectra[ROWS * s : ROWS * (s + 1)]
    first_channel = lax.broadcasted_iota(jnp.int32, gain_ref.shape, 0) % 2 == 0
    gain_ref[...] = jnp.where(first_channel, skip_ref[:, 0:1], skip_ref[:, 1:2])


def blocks_kernel(in_ref, there_ref, filter_there_ref, high_ref, low_ref, filter_high_ref, filter_low_ref, out_ref):
    half = lax.axis_index("ctx") // HALVES

    def spectra(table_ref, signals):
        cols = slice(PAIR * signals[0], PAIR * (signals[-1] + 1))
        high, low = split(jnp.concatenate([in_ref[n : n + 16, 0, cols] for n in range(0, BLOCKS, 16)], 0))
        terms = dot(table_ref[...], jnp.concatenate([high, high, low], 0))
        cosine, sine = terms[: 2 * BLOCKS], terms[2 * BLOCKS :]
        result = []
        for n in range(len(signals)):
            real, imag = slice(PAIR * n, PAIR * n + LANES), slice(PAIR * n + LANES, PAIR * (n + 1))
            result.append((cosine[:, real] + sine[:, imag], cosine[:, imag] - sine[:, real]))
        return result

    def blocks(table_high_ref, table_low_ref, values):
        cosine = jnp.concatenate([part for real, imag in values for part in (real, imag)], 1)
        sine = jnp.concatenate([part for real, imag in values for part in (-imag, real)], 1)
        high, low = split(jnp.concatenate([cosine, sine], 0))
        table_high = table_high_ref[half]
        both = dot(jnp.concatenate([table_high, table_low_ref[half]], 0), high)
        return both[:HALVES] + (dot(table_high, low) + both[HALVES:])

    ((taps_re, taps_im),) = spectra(filter_there_ref, [4])
    signals = spectra(there_ref, range(4))
    results, corr_re, corr_im = [], 0.0, 0.0
    for re, im in signals[:2]:
        results.append((taps_re * re - taps_im * im, taps_re * im + taps_im * re))
    for (mixed_re, mixed_im), (re, im) in zip(signals[:2], signals[2:]):
        results.append((taps_re * re + taps_im * im, taps_re * im - taps_im * re))
        corr_re += mixed_re * re + mixed_im * im
        corr_im += mixed_re * im - mixed_im * re
    out_ref[:, 0, : 4 * PAIR] = blocks(high_ref, low_ref, results)
    out_ref[:, 0, 4 * PAIR :] = blocks(filter_high_ref, filter_low_ref, [(corr_re, corr_im)])


def inverse_kernel(
    in_ref, query_ref, key_ref, values_ref, cot_ref, gain_ref, pair_ref, last_ref, twiddle_ref, high_ref, low_ref,
    out_ref, grad_query_ref, grad_key_ref, grad_values_ref, grad_filter_ref,
):
    f32, bf16 = jnp.float32, jnp.bfloat16
    spectra = jnp.concatenate([in_ref[:, 0, PAIR * s : PAIR * (s + 1)] for s in range(SIGNALS)], 0)
    spread = dot3(spectra, high_ref[...], low_ref[...])
    tw_re, tw_im = twiddle_ref[0], twiddle_ref[1]
    turned = []
    for s in range(SIGNALS):
        rows = slice(ROWS * s, ROWS * (s + 1))
        re, im = spread[rows, :LANES], spread[rows, LANES:]
        turned += [re * tw_re + im * tw_im, im * tw_re - re * tw_im]
    pairs = jnp.concatenate([jnp.concatenate(turned[:4], 0), jnp.concatenate(turned[4:8], 0)], 1)
    grad_filter = dot(last_ref[...], stack3(jnp.concatenate(turned[8:], 0)))
    for copy in range(grad_filter_ref.shape[0]):
        grad_filter_ref[copy] = grad_filter
    pairs = dot(pair_ref[...], stack3(pairs))
    query, cot = query_ref[...].astype(f32), cot_ref[...].astype(f32)
    key, value = key_ref[...].astype(f32), values_ref[...].astype(f32)
    gain = gain_ref[...]
    summed = pairs[:, :LANES] + gain * (key * value)
    out_ref[...] = (query * summed).astype(bf16)
    grad_query_ref[...] = (cot * summed).astype(bf16)
    grad_mixed = pairs[:, LANES:] + gain * (cot * query)
    grad_key_ref[...] = (grad_mixed * value).astype(bf16)
    grad_values_ref[...] = (grad_mixed * key).astype(bf16)


def finish_kernel(partials_ref, *refs):
    gated, outs, (total_ref, sems) = refs[:4], refs[4:9], refs[9:]
    copies = [pltpu.make_async_copy(src, dst, sems.at[n]) for n, (src, dst) in enumerate(zip((*gated, total_ref), outs))]
    for copy in copies[:4]:
        copy.start()
    total_ref[...] = jnp.sum(partials_ref[...], axis=0)
    copies[4].start()
    for copy in copies:
        copy.wait()


def by_rows(pair):
    return pair.reshape(2, ROWS, LANES).transpose(1, 0, 2).reshape(2 * ROWS, LANES)


def by_channel(rows):
    return rows.reshape(ROWS, 2, LANES).transpose(1, 0, 2).reshape(2, BLOCK)


def per_device(gate_q, gate_k, values, filter_taps, skip_gain, cotangent):
    f32 = jnp.float32
    first, last, twiddle, second, second_back = jax.tree.map(jnp.asarray, make_tables())
    groups = lax.axis_size("chan")
    gate_q, gate_k, values, cotangent = map(by_rows, (gate_q, gate_k, values, cotangent))
    operands = (gate_k, values, cotangent, gate_q, filter_taps.reshape(ROWS, LANES), *first, twiddle[0], *second, skip_gain[None])
    sent, gain = pl.pallas_call(
        forward_kernel,
        out_shape=(jax.ShapeDtypeStruct((BLOCKS, 1, WIDTH), f32), pltpu.VMEM(gate_q.shape, f32)),
        in_specs=[pl.BlockSpec(memory_space=pltpu.HBM)] * len(operands),
        scratch_shapes=[
            *(pltpu.VMEM(v.shape, v.dtype) for v in operands),
            pltpu.SemaphoreType.DMA((len(operands),)),
        ],
        compiler_params=SMALL,
        name="forward_transform",
    )(*(pltpu.with_memory_space_constraint(v, pltpu.HBM) for v in operands))
    blocks = lax.all_to_all(sent, "ctx", 0, 0, tiled=True, axis_index_groups=CTX_ORDER)
    sent = pl.pallas_call(
        blocks_kernel,
        out_shape=jax.ShapeDtypeStruct((HALVES, 1, WIDTH), f32),
        compiler_params=SMALL,
        name="block_convolutions",
    )(blocks, *jax.tree.map(jnp.asarray, make_block_tables()))
    spectra = lax.all_to_all(sent, "ctx", 0, 0, tiled=True, axis_index_groups=HALF_ORDER)
    like = pltpu.VMEM(gate_q.shape, jnp.bfloat16)
    *gated, partial_filter = pl.pallas_call(
        inverse_kernel,
        out_shape=(like, like, like, like, jax.ShapeDtypeStruct((groups, ROWS, LANES), f32)),
        compiler_params=SMALL,
        name="inverse_transform",
    )(spectra, gate_q, gate_k, values, cotangent, gain, *last, twiddle[1], *second_back)
    partials = lax.all_to_all(partial_filter, "chan", 0, 0, tiled=True, axis_index_groups=CHAN_ORDER)
    like = jax.ShapeDtypeStruct(gate_q.shape, jnp.bfloat16)
    *gated, grad_filter = pl.pallas_call(
        finish_kernel,
        out_shape=(like, like, like, like, jax.ShapeDtypeStruct((ROWS, LANES), f32)),
        out_specs=[pl.BlockSpec(memory_space=pltpu.HBM)] * 5,
        scratch_shapes=[pltpu.VMEM((ROWS, LANES), f32), pltpu.SemaphoreType.DMA((5,))],
        compiler_params=SMALL,
        name="finish",
    )(partials, *gated)
    return (*map(by_channel, gated), grad_filter.reshape(BLOCK))


def solution(mesh):
    return jax.shard_map(
        per_device,
        mesh=mesh,
        in_specs=(
            P("chan", "ctx"),
            P("chan", "ctx"),
            P("chan", "ctx"),
            P("ctx"),
            P("chan"),
            P("chan", "ctx"),
        ),
        out_specs=(
            P("chan", "ctx"),
            P("chan", "ctx"),
            P("chan", "ctx"),
            P("chan", "ctx"),
            P("ctx"),
        ),
        check_vma=False,
    )
```

```python
import numpy as np

import jax
import jax.numpy as jnp
from jax import lax
from jax.experimental import pallas as pl
from jax.experimental.pallas import tpu as pltpu
from jax.sharding import PartitionSpec as P

BLOCK = 4096
BLOCKS = 64
ROWS = 32
LANES = 128
HALVES = 32
SIGNALS = 5
PAIR = 2 * LANES
WIDTH = SIGNALS * PAIR
SMALL = pltpu.CompilerParams(vmem_limit_bytes=8 << 20)
def plane_order(corner):
    return [corner if p == 0 else 0 if p == corner else p for p in range(HALVES)]


FIRST_ORDER, SECOND_ORDER = plane_order(21), plane_order(20)
CTX_ORDER = [[HALVES + p for p in FIRST_ORDER] + FIRST_ORDER]
HALF_ORDER = [SECOND_ORDER, [HALVES + p for p in SECOND_ORDER]]
CHAN_ORDER = [[5, 4, 2, 3, 6, 7, 0, 1]]


def split(value):
    high = value.astype(jnp.bfloat16)
    return high, (value - high.astype(jnp.float32)).astype(jnp.bfloat16)


def split_table(table):
    high = table.astype(np.float32).astype(jnp.bfloat16)
    low = (table - high.astype(np.float64)).astype(np.float32).astype(jnp.bfloat16)
    return high, low


def make_tables():
    a = np.arange(ROWS)
    b = np.arange(LANES)
    first = np.exp(-2j * np.pi * (a[:, None] * a[None, :] / ROWS + LANES * a[None, :] / (4 * BLOCK)))
    first = np.concatenate([first.real, first.imag], 0)
    first_pair = np.zeros((2, 2 * ROWS, ROWS, 2))
    first_pair[0, :, :, 0] = first_pair[1, :, :, 1] = first
    k1 = np.array([FIRST_ORDER.index(p) for p in SECOND_ORDER])
    last = np.exp(2j * np.pi * (a[:, None] * k1[None, :] / ROWS + LANES * a[:, None] / (4 * BLOCK)))
    last = np.concatenate([last.real, -last.imag], 1) / BLOCK / (BLOCK * BLOCKS) ** 0.5
    last_pair = np.zeros((ROWS, 2, 2, 2 * ROWS))
    last_pair[:, 0, 0] = last_pair[:, 1, 1] = last

    def thrice(table):
        high, low = split_table(table)
        return np.concatenate([high, low, high], 1)

    first_table = thrice(first_pair.reshape(4 * ROWS, 2 * ROWS)), thrice(first)
    last_table = thrice(last_pair.reshape(2 * ROWS, 4 * ROWS)), thrice(last)
    twiddle = np.exp(-2j * np.pi * b[None, :] * (4 * a[:, None] + 1) / (4 * BLOCK))
    twiddle = np.stack([twiddle.real, twiddle.imag]).astype(np.float32)
    twiddle = twiddle, twiddle[:, k1]
    angle = 2 * np.pi * (b[:, None] * b[None, :] % LANES) / LANES
    cos, sin = np.cos(angle), np.sin(angle)
    second = np.block([[cos, -sin], [sin, cos]])
    return first_table, last_table, twiddle, split_table(second), split_table(second.T)


def make_block_tables():
    blocks = np.array(CTX_ORDER[0])
    results = np.array(HALF_ORDER)
    phases = np.arange(2 * BLOCKS)
    wave = np.exp(-2j * np.pi * phases[:, None] * blocks[None, :] / (2 * BLOCKS))
    step = np.exp(-2j * np.pi * phases / (2 * BLOCKS))
    back = np.exp(2j * np.pi * results[:, :, None] * phases / (2 * BLOCKS)) / (2 * BLOCKS)

    def there(table):
        high, low = split_table(np.concatenate([table.real, -table.imag], 0))
        return np.concatenate([high, low, high], 1)

    def here(table):
        return split_table(np.concatenate([table.real, table.imag], 2))

    filter_wave = wave * (1 + 1j * step)[:, None]
    filter_back = back * (1 - 1j * np.conj(step))
    return there(wave), there(filter_wave), *here(back), *here(filter_back)


def dot(left, right):
    return jnp.dot(left, right, preferred_element_type=jnp.float32)


def dot3(value, high, low):
    value_high, value_low = split(value)
    rows = value.shape[0]
    both = dot(jnp.concatenate([value_high, value_low], 0), high)
    return both[:rows] + (dot(value_high, low) + both[rows:])


def stack3(value):
    high, low = split(value)
    return jnp.concatenate([high, high, low], 0)


def forward_kernel(*refs):
    operands, (out_ref, gain_ref, *held, sems) = refs[:11], refs[11:]
    copies = [pltpu.make_async_copy(src, dst, sems.at[n]) for n, (src, dst) in enumerate(zip(operands, held))]
    for copy in copies[8:] + copies[:8]:
        copy.start()
    key_ref, values_ref, cot_ref, query_ref, taps_ref, pair_ref, first_ref, twiddle_ref, high_ref, low_ref, skip_ref = held
    f32 = jnp.float32
    for copy in copies[:5]:
        copy.wait()
    mixed = key_ref[...].astype(f32) * values_ref[...].astype(f32)
    grad = cot_ref[...].astype(f32) * query_ref[...].astype(f32)
    pairs, taps = stack3(jnp.concatenate([mixed, grad], 1)), stack3(taps_ref[...])
    for copy in copies[5:7]:
        copy.wait()
    pairs, taps = dot(pair_ref[...], pairs), dot(first_ref[...], taps)
    copies[7].wait()
    tw_re, tw_im = twiddle_ref[0], twiddle_ref[1]
    places = [(pairs, 0, 0), (pairs, 1, 0), (pairs, 0, 1), (pairs, 1, 1), (taps, 0, 0)]
    turned = []
    for spread, row, col in places:
        cols = slice(LANES * col, LANES * (col + 1))
        re = spread[2 * ROWS * row : 2 * ROWS * row + ROWS, cols]
        im = spread[2 * ROWS * row + ROWS : 2 * ROWS * (row + 1), cols]
        turned.append(jnp.concatenate([re * tw_re - im * tw_im, re * tw_im + im * tw_re], 1))
    for copy in copies[8:]:
        copy.wait()
    spectra = dot3(jnp.concatenate(turned, 0), high_ref[...], low_ref[...])
    for s in range(SIGNALS):
        for h in range(2):
            out_ref[HALVES * h : HALVES * (h + 1), 0, PAIR * s : PAIR * (s + 1)] = spectra[ROWS * s : ROWS * (s + 1)]
    first_channel = lax.broadcasted_iota(jnp.int32, gain_ref.shape, 0) % 2 == 0
    gain_ref[...] = jnp.where(first_channel, skip_ref[:, 0:1], skip_ref[:, 1:2])


def blocks_kernel(in_ref, there_ref, filter_there_ref, high_ref, low_ref, filter_high_ref, filter_low_ref, out_ref):
    half = lax.axis_index("ctx") // HALVES

    def spectra(table_ref, signals):
        cols = slice(PAIR * signals[0], PAIR * (signals[-1] + 1))
        high, low = split(jnp.concatenate([in_ref[n : n + 16, 0, cols] for n in range(0, BLOCKS, 16)], 0))
        terms = dot(table_ref[...], jnp.concatenate([high, high, low], 0))
        cosine, sine = terms[: 2 * BLOCKS], terms[2 * BLOCKS :]
        result = []
        for n in range(len(signals)):
            real, imag = slice(PAIR * n, PAIR * n + LANES), slice(PAIR * n + LANES, PAIR * (n + 1))
            result.append((cosine[:, real] + sine[:, imag], cosine[:, imag] - sine[:, real]))
        return result

    def blocks(table_high_ref, table_low_ref, values):
        cosine = jnp.concatenate([part for real, imag in values for part in (real, imag)], 1)
        sine = jnp.concatenate([part for real, imag in values for part in (-imag, real)], 1)
        high, low = split(jnp.concatenate([cosine, sine], 0))
        table_high = table_high_ref[half]
        both = dot(jnp.concatenate([table_high, table_low_ref[half]], 0), high)
        return both[:HALVES] + (dot(table_high, low) + both[HALVES:])

    ((taps_re, taps_im),) = spectra(filter_there_ref, [4])
    signals = spectra(there_ref, range(4))
    results, corr_re, corr_im = [], 0.0, 0.0
    for re, im in signals[:2]:
        results.append((taps_re * re - taps_im * im, taps_re * im + taps_im * re))
    for (mixed_re, mixed_im), (re, im) in zip(signals[:2], signals[2:]):
        results.append((taps_re * re + taps_im * im, taps_re * im - taps_im * re))
        corr_re += mixed_re * re + mixed_im * im
        corr_im += mixed_re * im - mixed_im * re
    out_ref[:, 0, : 4 * PAIR] = blocks(high_ref, low_ref, results)
    out_ref[:, 0, 4 * PAIR :] = blocks(filter_high_ref, filter_low_ref, [(corr_re, corr_im)])


def inverse_kernel(
    in_ref, query_ref, key_ref, values_ref, cot_ref, gain_ref, pair_ref, last_ref, twiddle_ref, high_ref, low_ref,
    out_ref, grad_query_ref, grad_key_ref, grad_values_ref, grad_filter_ref,
):
    f32, bf16 = jnp.float32, jnp.bfloat16
    spectra = jnp.concatenate([in_ref[:, 0, PAIR * s : PAIR * (s + 1)] for s in range(SIGNALS)], 0)
    spread = dot3(spectra, high_ref[...], low_ref[...])
    tw_re, tw_im = twiddle_ref[0], twiddle_ref[1]
    turned = []
    for s in range(SIGNALS):
        rows = slice(ROWS * s, ROWS * (s + 1))
        re, im = spread[rows, :LANES], spread[rows, LANES:]
        turned += [re * tw_re + im * tw_im, im * tw_re - re * tw_im]
    pairs = jnp.concatenate([jnp.concatenate(turned[:4], 0), jnp.concatenate(turned[4:8], 0)], 1)
    grad_filter = dot(last_ref[...], stack3(jnp.concatenate(turned[8:], 0)))
    for copy in range(grad_filter_ref.shape[0]):
        grad_filter_ref[copy] = grad_filter
    pairs = dot(pair_ref[...], stack3(pairs))
    query, cot = query_ref[...].astype(f32), cot_ref[...].astype(f32)
    key, value = key_ref[...].astype(f32), values_ref[...].astype(f32)
    gain = gain_ref[...]
    summed = pairs[:, :LANES] + gain * (key * value)
    out_ref[...] = (query * summed).astype(bf16)
    grad_query_ref[...] = (cot * summed).astype(bf16)
    grad_mixed = pairs[:, LANES:] + gain * (cot * query)
    grad_key_ref[...] = (grad_mixed * value).astype(bf16)
    grad_values_ref[...] = (grad_mixed * key).astype(bf16)


def finish_kernel(partials_ref, *refs):
    gated, outs, (total_ref, sems) = refs[:4], refs[4:9], refs[9:]
    copies = [pltpu.make_async_copy(src, dst, sems.at[n]) for n, (src, dst) in enumerate(zip((*gated, total_ref), outs))]
    for copy in copies[:4]:
        copy.start()
    total_ref[...] = jnp.sum(partials_ref[...], axis=0)
    copies[4].start()
    for copy in copies:
        copy.wait()


def by_rows(pair):
    return pair.reshape(2, ROWS, LANES).transpose(1, 0, 2).reshape(2 * ROWS, LANES)


def by_channel(rows):
    return rows.reshape(ROWS, 2, LANES).transpose(1, 0, 2).reshape(2, BLOCK)


def per_device(gate_q, gate_k, values, filter_taps, skip_gain, cotangent):
    f32 = jnp.float32
    first, last, twiddle, second, second_back = jax.tree.map(jnp.asarray, make_tables())
    groups = lax.axis_size("chan")
    gate_q, gate_k, values, cotangent = map(by_rows, (gate_q, gate_k, values, cotangent))
    operands = (gate_k, values, cotangent, gate_q, filter_taps.reshape(ROWS, LANES), *first, twiddle[0], *second, skip_gain[None])
    sent, gain = pl.pallas_call(
        forward_kernel,
        out_shape=(jax.ShapeDtypeStruct((BLOCKS, 1, WIDTH), f32), pltpu.VMEM(gate_q.shape, f32)),
        in_specs=[pl.BlockSpec(memory_space=pltpu.HBM)] * len(operands),
        scratch_shapes=[
            *(pltpu.VMEM(v.shape, v.dtype) for v in operands),
            pltpu.SemaphoreType.DMA((len(operands),)),
        ],
        compiler_params=SMALL,
        name="forward_transform",
    )(*(pltpu.with_memory_space_constraint(v, pltpu.HBM) for v in operands))
    blocks = lax.all_to_all(sent, "ctx", 0, 0, tiled=True, axis_index_groups=CTX_ORDER)
    sent = pl.pallas_call(
        blocks_kernel,
        out_shape=jax.ShapeDtypeStruct((HALVES, 1, WIDTH), f32),
        compiler_params=SMALL,
        name="block_convolutions",
    )(blocks, *jax.tree.map(jnp.asarray, make_block_tables()))
    spectra = lax.all_to_all(sent, "ctx", 0, 0, tiled=True, axis_index_groups=HALF_ORDER)
    like = pltpu.VMEM(gate_q.shape, jnp.bfloat16)
    *gated, partial_filter = pl.pallas_call(
        inverse_kernel,
        out_shape=(like, like, like, like, jax.ShapeDtypeStruct((groups, ROWS, LANES), f32)),
        compiler_params=SMALL,
        name="inverse_transform",
    )(spectra, gate_q, gate_k, values, cotangent, gain, *last, twiddle[1], *second_back)
    partials = lax.all_to_all(partial_filter, "chan", 0, 0, tiled=True, axis_index_groups=CHAN_ORDER)
    like = jax.ShapeDtypeStruct(gate_q.shape, jnp.bfloat16)
    *gated, grad_filter = pl.pallas_call(
        finish_kernel,
        out_shape=(like, like, like, like, jax.ShapeDtypeStruct((ROWS, LANES), f32)),
        out_specs=[pl.BlockSpec(memory_space=pltpu.HBM)] * 5,
        scratch_shapes=[pltpu.VMEM((ROWS, LANES), f32), pltpu.SemaphoreType.DMA((5,))],
        compiler_params=SMALL,
        name="finish",
    )(partials, *gated)
    return (*map(by_channel, gated), grad_filter.reshape(BLOCK))


def solution(mesh):
    return jax.shard_map(
        per_device,
        mesh=mesh,
        in_specs=(
            P("chan", "ctx"),
            P("chan", "ctx"),
            P("chan", "ctx"),
            P("ctx"),
            P("chan"),
            P("chan", "ctx"),
        ),
        out_specs=(
            P("chan", "ctx"),
            P("chan", "ctx"),
            P("chan", "ctx"),
            P("chan", "ctx"),
            P("ctx"),
        ),
        check_vma=False,
    )
```

```python
import numpy as np

import jax
import jax.numpy as jnp
from jax import lax
from jax.experimental import pallas as pl
from jax.experimental.pallas import tpu as pltpu
from jax.sharding import PartitionSpec as P

BLOCK = 4096
BLOCKS = 64
ROWS = 32
LANES = 128
HALVES = 32
SIGNALS = 5
PAIR = 2 * LANES
WIDTH = SIGNALS * PAIR
SMALL = pltpu.CompilerParams(vmem_limit_bytes=8 << 20)
def plane_order(corner):
    return [corner if p == 0 else 0 if p == corner else p for p in range(HALVES)]


FIRST_ORDER, SECOND_ORDER = plane_order(21), plane_order(19)
CTX_ORDER = [[HALVES + p for p in FIRST_ORDER] + FIRST_ORDER]
HALF_ORDER = [SECOND_ORDER, [HALVES + p for p in SECOND_ORDER]]
CHAN_ORDER = [[5, 4, 2, 3, 6, 7, 0, 1]]


def split(value):
    high = value.astype(jnp.bfloat16)
    return high, (value - high.astype(jnp.float32)).astype(jnp.bfloat16)


def split_table(table):
    high = table.astype(np.float32).astype(jnp.bfloat16)
    low = (table - high.astype(np.float64)).astype(np.float32).astype(jnp.bfloat16)
    return high, low


def make_tables():
    a = np.arange(ROWS)
    b = np.arange(LANES)
    first = np.exp(-2j * np.pi * (a[:, None] * a[None, :] / ROWS + LANES * a[None, :] / (4 * BLOCK)))
    first = np.concatenate([first.real, first.imag], 0)
    first_pair = np.zeros((2, 2 * ROWS, ROWS, 2))
    first_pair[0, :, :, 0] = first_pair[1, :, :, 1] = first
    k1 = np.array([FIRST_ORDER.index(p) for p in SECOND_ORDER])
    last = np.exp(2j * np.pi * (a[:, None] * k1[None, :] / ROWS + LANES * a[:, None] / (4 * BLOCK)))
    last = np.concatenate([last.real, -last.imag], 1) / BLOCK / (BLOCK * BLOCKS) ** 0.5
    last_pair = np.zeros((ROWS, 2, 2, 2 * ROWS))
    last_pair[:, 0, 0] = last_pair[:, 1, 1] = last

    def thrice(table):
        high, low = split_table(table)
        return np.concatenate([high, low, high], 1)

    first_table = thrice(first_pair.reshape(4 * ROWS, 2 * ROWS)), thrice(first)
    last_table = thrice(last_pair.reshape(2 * ROWS, 4 * ROWS)), thrice(last)
    twiddle = np.exp(-2j * np.pi * b[None, :] * (4 * a[:, None] + 1) / (4 * BLOCK))
    twiddle = np.stack([twiddle.real, twiddle.imag]).astype(np.float32)
    twiddle = twiddle, twiddle[:, k1]
    angle = 2 * np.pi * (b[:, None] * b[None, :] % LANES) / LANES
    cos, sin = np.cos(angle), np.sin(angle)
    second = np.block([[cos, -sin], [sin, cos]])
    return first_table, last_table, twiddle, split_table(second), split_table(second.T)


def make_block_tables():
    blocks = np.array(CTX_ORDER[0])
    results = np.array(HALF_ORDER)
    phases = np.arange(2 * BLOCKS)
    wave = np.exp(-2j * np.pi * phases[:, None] * blocks[None, :] / (2 * BLOCKS))
    step = np.exp(-2j * np.pi * phases / (2 * BLOCKS))
    back = np.exp(2j * np.pi * results[:, :, None] * phases / (2 * BLOCKS)) / (2 * BLOCKS)

    def there(table):
        high, low = split_table(np.concatenate([table.real, -table.imag], 0))
        return np.concatenate([high, low, high], 1)

    def here(table):
        return split_table(np.concatenate([table.real, table.imag], 2))

    filter_wave = wave * (1 + 1j * step)[:, None]
    filter_back = back * (1 - 1j * np.conj(step))
    return there(wave), there(filter_wave), *here(back), *here(filter_back)


def dot(left, right):
    return jnp.dot(left, right, preferred_element_type=jnp.float32)


def dot3(value, high, low):
    value_high, value_low = split(value)
    rows = value.shape[0]
    both = dot(jnp.concatenate([value_high, value_low], 0), high)
    return both[:rows] + (dot(value_high, low) + both[rows:])


def stack3(value):
    high, low = split(value)
    return jnp.concatenate([high, high, low], 0)


def forward_kernel(*refs):
    operands, (out_ref, gain_ref, *held, sems) = refs[:11], refs[11:]
    copies = [pltpu.make_async_copy(src, dst, sems.at[n]) for n, (src, dst) in enumerate(zip(operands, held))]
    for copy in copies:
        copy.start()
    key_ref, values_ref, cot_ref, query_ref, taps_ref, pair_ref, first_ref, twiddle_ref, high_ref, low_ref, skip_ref = held
    f32 = jnp.float32
    for copy in copies[:5]:
        copy.wait()
    mixed = key_ref[...].astype(f32) * values_ref[...].astype(f32)
    grad = cot_ref[...].astype(f32) * query_ref[...].astype(f32)
    pairs, taps = stack3(jnp.concatenate([mixed, grad], 1)), stack3(taps_ref[...])
    for copy in copies[5:7]:
        copy.wait()
    pairs, taps = dot(pair_ref[...], pairs), dot(first_ref[...], taps)
    copies[7].wait()
    tw_re, tw_im = twiddle_ref[0], twiddle_ref[1]
    places = [(pairs, 0, 0), (pairs, 1, 0), (pairs, 0, 1), (pairs, 1, 1), (taps, 0, 0)]
    turned = []
    for spread, row, col in places:
        cols = slice(LANES * col, LANES * (col + 1))
        re = spread[2 * ROWS * row : 2 * ROWS * row + ROWS, cols]
        im = spread[2 * ROWS * row + ROWS : 2 * ROWS * (row + 1), cols]
        turned.append(jnp.concatenate([re * tw_re - im * tw_im, re * tw_im + im * tw_re], 1))
    for copy in copies[8:]:
        copy.wait()
    spectra = dot3(jnp.concatenate(turned, 0), high_ref[...], low_ref[...])
    for s in range(SIGNALS):
        for h in range(2):
            out_ref[HALVES * h : HALVES * (h + 1), 0, PAIR * s : PAIR * (s + 1)] = spectra[ROWS * s : ROWS * (s + 1)]
    first_channel = lax.broadcasted_iota(jnp.int32, gain_ref.shape, 0) % 2 == 0
    gain_ref[...] = jnp.where(first_channel, skip_ref[:, 0:1], skip_ref[:, 1:2])


def blocks_kernel(in_ref, there_ref, filter_there_ref, high_ref, low_ref, filter_high_ref, filter_low_ref, out_ref):
    half = lax.axis_index("ctx") // HALVES

    def spectra(table_ref, signals):
        cols = slice(PAIR * signals[0], PAIR * (signals[-1] + 1))
        high, low = split(jnp.concatenate([in_ref[n : n + 16, 0, cols] for n in range(0, BLOCKS, 16)], 0))
        terms = dot(table_ref[...], jnp.concatenate([high, high, low], 0))
        cosine, sine = terms[: 2 * BLOCKS], terms[2 * BLOCKS :]
        result = []
        for n in range(len(signals)):
            real, imag = slice(PAIR * n, PAIR * n + LANES), slice(PAIR * n + LANES, PAIR * (n + 1))
            result.append((cosine[:, real] + sine[:, imag], cosine[:, imag] - sine[:, real]))
        return result

    def blocks(table_high_ref, table_low_ref, values):
        cosine = jnp.concatenate([part for real, imag in values for part in (real, imag)], 1)
        sine = jnp.concatenate([part for real, imag in values for part in (-imag, real)], 1)
        high, low = split(jnp.concatenate([cosine, sine], 0))
        table_high = table_high_ref[half]
        both = dot(jnp.concatenate([table_high, table_low_ref[half]], 0), high)
        return both[:HALVES] + (dot(table_high, low) + both[HALVES:])

    ((taps_re, taps_im),) = spectra(filter_there_ref, [4])
    signals = spectra(there_ref, range(4))
    results, corr_re, corr_im = [], 0.0, 0.0
    for re, im in signals[:2]:
        results.append((taps_re * re - taps_im * im, taps_re * im + taps_im * re))
    for (mixed_re, mixed_im), (re, im) in zip(signals[:2], signals[2:]):
        results.append((taps_re * re + taps_im * im, taps_re * im - taps_im * re))
        corr_re += mixed_re * re + mixed_im * im
        corr_im += mixed_re * im - mixed_im * re
    out_ref[:, 0, : 4 * PAIR] = blocks(high_ref, low_ref, results)
    out_ref[:, 0, 4 * PAIR :] = blocks(filter_high_ref, filter_low_ref, [(corr_re, corr_im)])


def inverse_kernel(
    in_ref, query_ref, key_ref, values_ref, cot_ref, gain_ref, pair_ref, last_ref, twiddle_ref, high_ref, low_ref,
    out_ref, grad_query_ref, grad_key_ref, grad_values_ref, grad_filter_ref,
):
    f32, bf16 = jnp.float32, jnp.bfloat16
    spectra = jnp.concatenate([in_ref[:, 0, PAIR * s : PAIR * (s + 1)] for s in range(SIGNALS)], 0)
    spread = dot3(spectra, high_ref[...], low_ref[...])
    tw_re, tw_im = twiddle_ref[0], twiddle_ref[1]
    turned = []
    for s in range(SIGNALS):
        rows = slice(ROWS * s, ROWS * (s + 1))
        re, im = spread[rows, :LANES], spread[rows, LANES:]
        turned += [re * tw_re + im * tw_im, im * tw_re - re * tw_im]
    pairs = jnp.concatenate([jnp.concatenate(turned[:4], 0), jnp.concatenate(turned[4:8], 0)], 1)
    grad_filter = dot(last_ref[...], stack3(jnp.concatenate(turned[8:], 0)))
    for copy in range(grad_filter_ref.shape[0]):
        grad_filter_ref[copy] = grad_filter
    pairs = dot(pair_ref[...], stack3(pairs))
    query, cot = query_ref[...].astype(f32), cot_ref[...].astype(f32)
    key, value = key_ref[...].astype(f32), values_ref[...].astype(f32)
    gain = gain_ref[...]
    summed = pairs[:, :LANES] + gain * (key * value)
    out_ref[...] = (query * summed).astype(bf16)
    grad_query_ref[...] = (cot * summed).astype(bf16)
    grad_mixed = pairs[:, LANES:] + gain * (cot * query)
    grad_key_ref[...] = (grad_mixed * value).astype(bf16)
    grad_values_ref[...] = (grad_mixed * key).astype(bf16)


def finish_kernel(partials_ref, *refs):
    gated, outs, (total_ref, sems) = refs[:4], refs[4:9], refs[9:]
    copies = [pltpu.make_async_copy(src, dst, sems.at[n]) for n, (src, dst) in enumerate(zip((*gated, total_ref), outs))]
    for copy in copies[:4]:
        copy.start()
    total_ref[...] = jnp.sum(partials_ref[...], axis=0)
    copies[4].start()
    for copy in copies:
        copy.wait()


def by_rows(pair):
    return pair.reshape(2, ROWS, LANES).transpose(1, 0, 2).reshape(2 * ROWS, LANES)


def by_channel(rows):
    return rows.reshape(ROWS, 2, LANES).transpose(1, 0, 2).reshape(2, BLOCK)


def per_device(gate_q, gate_k, values, filter_taps, skip_gain, cotangent):
    f32 = jnp.float32
    first, last, twiddle, second, second_back = jax.tree.map(jnp.asarray, make_tables())
    groups = lax.axis_size("chan")
    gate_q, gate_k, values, cotangent = map(by_rows, (gate_q, gate_k, values, cotangent))
    operands = (gate_k, values, cotangent, gate_q, filter_taps.reshape(ROWS, LANES), *first, twiddle[0], *second, skip_gain[None])
    sent, gain = pl.pallas_call(
        forward_kernel,
        out_shape=(jax.ShapeDtypeStruct((BLOCKS, 1, WIDTH), f32), pltpu.VMEM(gate_q.shape, f32)),
        in_specs=[pl.BlockSpec(memory_space=pltpu.HBM)] * len(operands),
        scratch_shapes=[
            *(pltpu.VMEM(v.shape, v.dtype) for v in operands),
            pltpu.SemaphoreType.DMA((len(operands),)),
        ],
        compiler_params=SMALL,
        name="forward_transform",
    )(*(pltpu.with_memory_space_constraint(v, pltpu.HBM) for v in operands))
    blocks = lax.all_to_all(sent, "ctx", 0, 0, tiled=True, axis_index_groups=CTX_ORDER)
    sent = pl.pallas_call(
        blocks_kernel,
        out_shape=jax.ShapeDtypeStruct((HALVES, 1, WIDTH), f32),
        compiler_params=SMALL,
        name="block_convolutions",
    )(blocks, *jax.tree.map(jnp.asarray, make_block_tables()))
    spectra = lax.all_to_all(sent, "ctx", 0, 0, tiled=True, axis_index_groups=HALF_ORDER)
    like = pltpu.VMEM(gate_q.shape, jnp.bfloat16)
    *gated, partial_filter = pl.pallas_call(
        inverse_kernel,
        out_shape=(like, like, like, like, jax.ShapeDtypeStruct((groups, ROWS, LANES), f32)),
        compiler_params=SMALL,
        name="inverse_transform",
    )(spectra, gate_q, gate_k, values, cotangent, gain, *last, twiddle[1], *second_back)
    partials = lax.all_to_all(partial_filter, "chan", 0, 0, tiled=True, axis_index_groups=CHAN_ORDER)
    like = jax.ShapeDtypeStruct(gate_q.shape, jnp.bfloat16)
    *gated, grad_filter = pl.pallas_call(
        finish_kernel,
        out_shape=(like, like, like, like, jax.ShapeDtypeStruct((ROWS, LANES), f32)),
        out_specs=[pl.BlockSpec(memory_space=pltpu.HBM)] * 5,
        scratch_shapes=[pltpu.VMEM((ROWS, LANES), f32), pltpu.SemaphoreType.DMA((5,))],
        compiler_params=SMALL,
        name="finish",
    )(partials, *gated)
    return (*map(by_channel, gated), grad_filter.reshape(BLOCK))


def solution(mesh):
    return jax.shard_map(
        per_device,
        mesh=mesh,
        in_specs=(
            P("chan", "ctx"),
            P("chan", "ctx"),
            P("chan", "ctx"),
            P("ctx"),
            P("chan"),
            P("chan", "ctx"),
        ),
        out_specs=(
            P("chan", "ctx"),
            P("chan", "ctx"),
            P("chan", "ctx"),
            P("chan", "ctx"),
            P("ctx"),
        ),
        check_vma=False,
    )
```
